32 devices in a mesh: seq: 8 (over z, y), expert: 4 (over x, core).
Axes of the slice: x: 2, y: 2, z: 4, core: 2. Of those that a mesh axis runs over, the one named last changes fastest.
Arguments:
- tokens: bfloat16 [1024, 4096], P('seq'), may hold values from -6 to 6
- expert_ids: int32 [1024, 8], P('seq'), may hold values from 0 to 15, all different within a row; in each aligned block of 128 rows (0 to 127, 128 to 255, ...) at most 96 rows name the same one
- route_weights: float32 [1024, 8], P('seq'), may hold values from 0.1 to 1
- w_gate: bfloat16 [32, 384, 4096], P(('seq', 'expert')), may hold values from -0.09375 to 0.09375
- w_up: bfloat16 [32, 384, 4096], P(('seq', 'expert')), may hold values from -0.09375 to 0.09375
- w_down: bfloat16 [32, 384, 4096], P(('seq', 'expert')), may hold values from -0.21875 to 0.21875
- query_rows: bfloat16 [1024, 8192], P('seq'), may hold values from -200 to 200
- key_rows: bfloat16 [1024, 512], P('seq'), may hold values from -7 to 7
- value_rows: bfloat16 [1024, 512], P('seq'), may hold values from -6 to 6
Outputs:
- moe_mixed: bfloat16 [1024, 4096], P('seq', 'expert')
- attn_out: bfloat16 [1024, 8192], P('expert', 'seq')
The draws below stay inside these ranges and needn't reach their ends.
Inputs may be any that keep to these rules, and one draw needn't show every extreme that they name: `expert_ids`: each token names 8 different experts. Among the 128 tokens of one index of seq no expert is named more than 96 times, and in some such block an expert is named exactly 96 times.
All inputs are finite; a program needn't handle non-finite values.
Results may differ from the reference program's by a relative error of at most 0.0085.
Values may be sent and summed in bfloat16 or wider, within the bound.
No kernel may reach another device: no remote copies, remote signals or barrier semaphores. Data moves between devices by JAX's collectives and lax.ppermute only.
A program may use at most 128 MiB of HBM per device.

```python
import math
import jax
import jax.numpy as jnp
import numpy as np
from jax import lax

D = 4096
HID = 768
TOPK = 8
HQ = 64
KVH = 4
HD = 128
BAND = 1024
TOK_DEV = 128
TOKENS = 1024
EXPERTS = 16
SLICES = 2
CAP = 96
N_SEQ = 8


def qk_pair(key):
    base = jax.random.fold_in(key, 11)
    key_query, key_key = jax.random.split(base, 2)
    query_part = jax.random.truncated_normal(key_query, -6.0, 6.0, (TOKENS, HQ, HD), jnp.float32)
    key_part = jax.random.truncated_normal(key_key, -6.0, 6.0, (TOKENS, KVH, HD), jnp.float32)
    return (query_part.reshape(TOKENS, HQ * HD), key_part.reshape(TOKENS, KVH * HD))


def draw_query_rows(key, part):
    return qk_pair(key)[0].astype(jnp.bfloat16)


def draw_key_rows(key, part):
    return qk_pair(key)[1].astype(jnp.bfloat16)


def steps_of(rng, extent, pieces, low, high):
    gain, own = 1.0, jax.random.fold_in(rng, 6)
    for position, blocks in pieces:
        steps = jnp.exp(jax.random.uniform(jax.random.fold_in(own, position), (blocks,), jnp.float32, low / len(pieces), high / len(pieces)))
        gain = gain * jnp.repeat(steps, extent[position] // blocks).reshape([-1 if axis == position else 1 for axis in range(len(extent))])
    return gain


def shared_out(own_key, own, number, rows, number_of, top, most, lean):
    ranking = jax.random.permutation(own_key, number_of)
    packed, ordinary = shares(number_of, rows * top, most, lean, True), shares(number_of, rows * top, most, lean, False)
    places = jnp.arange(number_of)

    def named(sizes, rotation):
        used = int((sizes > 0).sum())
        fixed = max(1, used // 4)
        moved = fixed + (places - fixed + rotation * (used - fixed)) % max(1, number_of - fixed)
        return jnp.zeros((number_of,), jnp.int32).at[ranking[jnp.where(places < fixed, places, moved)]].set(jnp.asarray(sizes, jnp.int32))

    sizes = jnp.where(number % 4 == 0, named(packed, number // 4), named(ordinary, number - number // 4 - 1))
    mixed = jax.random.permutation(jax.random.fold_in(own, 3), number_of)
    source_of, taker = mixed[0:number_of // 2 * 2:2], mixed[1:number_of // 2 * 2:2]
    margin = jnp.minimum(sizes[source_of] - 1, most - sizes[taker]) // 2
    margin = jnp.where((source_of == ranking[0]) | (taker == ranking[0]) | (sizes[taker] == 0), 0, jnp.maximum(margin, 0))
    moved = jax.random.randint(jax.random.fold_in(own, 4), (number_of // 2,), 0, 1 << 20) % (margin + 1)
    sizes = sizes.at[source_of].add(-moved).at[taker].add(moved)
    members = jnp.searchsorted(jnp.cumsum(sizes), jnp.arange(rows * top), side="right").astype(jnp.int32)
    table = members.reshape(top, rows).T
    table = table[jax.random.permutation(jax.random.fold_in(own, 1), rows)]
    rotation = jax.random.randint(jax.random.fold_in(own, 2), (rows, 1), 0, top)
    return jnp.take_along_axis(table, (jnp.arange(top)[None, :] + rotation) % top, axis=1)


def shares(amount, total, bound, lean, full):
    weights = [(1 << 20) // math.isqrt(rank ** lean) + 1 for rank in range(1, amount + 1)]
    largest = bound if full else min(bound, max(-(-total // amount), total * weights[0] // sum(weights)))
    least = 1 if total - largest >= amount - 1 else 0
    holding, rest = [largest] + [least] * (amount - 1), total - largest - least * (amount - 1)
    while rest > 0:
        candidates = [i for i in range(1, amount) if holding[i] < largest] or [i for i in range(1, amount) if holding[i] < bound]
        pool, remaining = sum([weights[i] for i in candidates]), rest
        for i in candidates:
            addition = min(bound - holding[i], max(1, remaining * weights[i] // pool), rest)
            holding[i] = holding[i] + addition
            rest = rest - addition
    return np.array(holding)


def scatter_about(key, shape, scale, reach, cuts=(), kind=jnp.bfloat16):
    entries = jax.random.normal(key, shape, jnp.float32) * scale
    if len(cuts) > 0:
        entries = steps_of(key, shape, cuts, -0.22, 0.18) * entries
    return jnp.clip(entries, min=-reach, max=reach).astype(kind)


def setup_inputs(seed: int = 0) -> dict:
    arg_keys = jax.random.split(jax.random.key(seed), 10)
    tokens = scatter_about(arg_keys[0], (TOKENS, D), 1.0, 6.0, ((0, 8),))
    expert_ids_keys = jax.random.split(jax.random.fold_in(arg_keys[1], 1), TOKENS // TOK_DEV)
    expert_ids_turns = jax.random.permutation(jax.random.fold_in(arg_keys[1], 3), TOKENS // TOK_DEV)
    expert_ids = jax.vmap(lambda own, number: shared_out(jax.random.fold_in(arg_keys[1], 2), own, number, TOK_DEV, EXPERTS, TOPK, CAP, 1))(expert_ids_keys, expert_ids_turns).reshape((TOKENS, TOPK))
    route_weights = jnp.clip(0.1 + 0.9 * jax.random.uniform(arg_keys[2], (TOKENS, TOPK), jnp.float32) ** steps_of(arg_keys[2], (TOKENS, TOPK), ((0, 8),), -0.2, 0.2), 0.1, 1.0)
    w_gate = scatter_about(arg_keys[3], (EXPERTS * SLICES, HID // SLICES, D), D ** -0.5, 0.09375, ((0, 32),))
    w_up = scatter_about(arg_keys[4], (EXPERTS * SLICES, HID // SLICES, D), D ** -0.5, 0.09375, ((0, 32),))
    w_down = scatter_about(arg_keys[5], (EXPERTS * SLICES, HID // SLICES, D), HID ** -0.5, 0.21875, ((0, 32),))
    query_rows = draw_query_rows(jax.random.fold_in(arg_keys[9], 71), 0)
    key_rows = draw_key_rows(jax.random.fold_in(arg_keys[9], 71), 0)
    value_rows = scatter_about(arg_keys[8], (TOKENS, KVH * HD), 1.0, 6.0, ((0, 8),))
    return dict(tokens=tokens, expert_ids=expert_ids, route_weights=route_weights, w_gate=w_gate, w_up=w_up, w_down=w_down, query_rows=query_rows, key_rows=key_rows, value_rows=value_rows)


def reference(tokens, expert_ids, route_weights, w_gate, w_up, w_down, query_rows, key_rows, value_rows):
    norm_weights = (route_weights / jnp.sum(route_weights, axis=1, keepdims=True)).astype(jnp.bfloat16)
    flat_ids = expert_ids.reshape(-1)
    flat_weights = norm_weights.reshape(-1).astype(jnp.float32)
    capacity_rows = N_SEQ * CAP

    def one_expert(accum, expert):
        member = flat_ids == expert
        positions = jnp.nonzero(member, size=capacity_rows, fill_value=0)[0].astype(jnp.int32)
        is_valid = jnp.arange(capacity_rows, dtype=jnp.int32) < jnp.sum(member.astype(jnp.int32))
        token_pos = positions // TOPK
        chosen = tokens[token_pos]
        summed = jnp.zeros((capacity_rows, D), jnp.float32)
        for slice_num in range(SLICES):
            slice_id = expert * SLICES + slice_num
            gate_rows = lax.dynamic_index_in_dim(w_gate, slice_id, 0, keepdims=False)
            up_rows = lax.dynamic_index_in_dim(w_up, slice_id, 0, keepdims=False)
            down_rows = lax.dynamic_index_in_dim(w_down, slice_id, 0, keepdims=False)
            gate_out = lax.dot_general(chosen, gate_rows, (((1,), (1,)), ((), ())), preferred_element_type=jnp.float32)
            up_out = lax.dot_general(chosen, up_rows, (((1,), (1,)), ((), ())), preferred_element_type=jnp.float32)
            hidden = (jax.nn.silu(gate_out) * up_out).astype(jnp.bfloat16)
            partial_value = jnp.dot(hidden, down_rows, preferred_element_type=jnp.float32).astype(jnp.bfloat16)
            summed = summed + partial_value.astype(jnp.float32)
        weight = jnp.where(is_valid, flat_weights[positions], jnp.float32(0.0))
        return accum.at[token_pos].add(weight[:, None] * summed), None

    accum = lax.scan(one_expert, jnp.zeros((TOKENS, D), jnp.float32), jnp.arange(EXPERTS, dtype=jnp.int32))[0]
    moe_mixed = accum.astype(jnp.bfloat16)

    group = HQ // KVH
    q_heads = query_rows.reshape(TOKENS, HQ, HD)
    k_heads = key_rows.reshape(TOKENS, KVH, HD)
    v_heads = value_rows.reshape(TOKENS, KVH, HD)
    positions = jnp.arange(TOKENS, dtype=jnp.int32)
    allowed = (positions[None, :] <= positions[:, None]) & (positions[None, :] > positions[:, None] - BAND)

    def one_head(head_id):
        query_mat = lax.dynamic_index_in_dim(q_heads, head_id, 1, keepdims=False)
        kv_id = head_id // group
        key_mat = lax.dynamic_index_in_dim(k_heads, kv_id, 1, keepdims=False)
        value_mat = lax.dynamic_index_in_dim(v_heads, kv_id, 1, keepdims=False)
        scores = jnp.dot(query_mat, key_mat.T, preferred_element_type=jnp.float32) * (HD ** -0.5)
        scores = jnp.where(allowed, scores, -jnp.inf)
        attn_probs = jax.nn.softmax(scores, axis=-1).astype(jnp.bfloat16)
        return jnp.dot(attn_probs, value_mat, preferred_element_type=jnp.float32).astype(jnp.bfloat16)

    heads_out = lax.map(one_head, jnp.arange(HQ, dtype=jnp.int32))
    attn_out = jnp.transpose(heads_out, (1, 0, 2)).reshape(TOKENS, HQ * HD)
    return moe_mixed, attn_out
```

```python
import jax
import jax.numpy as jnp
from jax import lax
from jax.sharding import PartitionSpec as P

HD = 128
BAND = 1024
EXP_SEQ = 2
AXES = ("seq", "expert")
BF = jnp.bfloat16
F32 = jnp.float32


def general_body(
    tokens, expert_ids, route_weights, w_gate, w_up, w_down, query_rows, key_rows, value_rows
):
    seq_index = lax.axis_index("seq")
    expert_index = lax.axis_index("expert")
    seq_count = lax.axis_size("seq")
    expert_count = lax.axis_size("expert")
    slice_count = expert_count // EXP_SEQ
    half_index = expert_index // slice_count
    tok_rows, width = tokens.shape
    route_count = expert_ids.shape[1]
    capacity = 3 * tok_rows * route_count // (2 * EXP_SEQ * seq_count)
    norm_weights = (route_weights / jnp.sum(route_weights, axis=1, keepdims=True)).astype(BF)
    targets = jnp.arange(seq_count, dtype=jnp.int32) * EXP_SEQ + half_index
    matched = expert_ids[:, :, None] == targets[None, None, :]
    routed_hit = jnp.sum(matched.astype(F32), axis=1)
    picked = jnp.sum(
        jnp.where(matched, norm_weights.astype(F32)[:, :, None], jnp.float32(0.0)), axis=1
    )
    row_ids = jnp.arange(tok_rows, dtype=jnp.int32)
    earlier = (row_ids[:, None] > row_ids[None, :]).astype(F32)
    slot_rank = jnp.dot(earlier, routed_hit, precision=lax.Precision.HIGHEST)
    slot_ids = jnp.arange(capacity, dtype=F32)
    onehot = (slot_rank.T[:, None, :] == slot_ids[None, :, None]) & (
        routed_hit.T[:, None, :] > 0.5
    )
    selector = onehot.astype(BF)
    outgoing = jnp.einsum("jct,td->jcd", selector, tokens, preferred_element_type=F32).astype(BF)
    incoming = lax.all_to_all(outgoing, "seq", split_axis=0, concat_axis=0, tiled=True)
    slot_count = incoming.shape[1]
    flat_rows = incoming.reshape(-1, width)
    nt = (((1,), (1,)), ((), ()))
    gate_out = lax.dot_general(flat_rows, w_gate[0], nt, preferred_element_type=F32)
    up_out = lax.dot_general(flat_rows, w_up[0], nt, preferred_element_type=F32)
    hidden = (jax.nn.silu(gate_out) * up_out).astype(BF)
    partial_value = jnp.dot(hidden, w_down[0], preferred_element_type=F32).astype(BF)
    partial_value = partial_value.reshape(seq_count, slot_count, width)
    returned = lax.all_to_all(partial_value, "seq", split_axis=0, concat_axis=0, tiled=True)
    combine = (onehot.astype(F32) * picked.T[:, None, :]).astype(BF)
    local_term = jnp.einsum("jct,jcd->td", combine, returned, preferred_element_type=F32)
    moe_mixed = lax.psum_scatter(local_term, "expert", scatter_dimension=1, tiled=True).astype(BF)
    head_total = query_rows.shape[1] // HD
    kv_heads = key_rows.shape[1] // HD
    heads_dev = head_total // seq_count
    block_rows = tok_rows * seq_count // expert_count
    block_start = expert_index * block_rows
    q_all = lax.all_to_all(query_rows, "seq", split_axis=1, concat_axis=0, tiled=True)
    q_block = lax.dynamic_slice_in_dim(q_all, block_start, block_rows, 0).reshape(
        block_rows, heads_dev, HD
    )
    k_full = lax.all_gather(key_rows, "seq", axis=0, tiled=True)
    v_full = lax.all_gather(value_rows, "seq", axis=0, tiled=True)
    kv_head = seq_index * heads_dev // (head_total // kv_heads)
    k_all = lax.dynamic_slice_in_dim(k_full, kv_head * HD, HD, 1)
    v_all = lax.dynamic_slice_in_dim(v_full, kv_head * HD, HD, 1)
    key_pad = jnp.zeros((BAND, HD), BF)
    k_window = lax.dynamic_slice_in_dim(
        jnp.concatenate([key_pad, k_all], axis=0), block_start, BAND + block_rows, 0
    )
    v_window = lax.dynamic_slice_in_dim(
        jnp.concatenate([key_pad, v_all], axis=0), block_start, BAND + block_rows, 0
    )
    query_pos = block_start + jnp.arange(block_rows, dtype=jnp.int32)
    key_pos = block_start - BAND + jnp.arange(BAND + block_rows, dtype=jnp.int32)
    allowed = (
        (key_pos[None, :] <= query_pos[:, None])
        & (key_pos[None, :] > query_pos[:, None] - BAND)
        & (key_pos[None, :] >= 0)
    )
    scores = jnp.einsum("qhd,kd->hqk", q_block, k_window, preferred_element_type=F32) * HD ** (-0.5)
    scores = jnp.where(allowed[None, :, :], scores, -jnp.inf)
    attn_probs = jax.nn.softmax(scores, axis=-1).astype(BF)
    attn_out = jnp.einsum(
        "hqk,kd->qhd", attn_probs, v_window, preferred_element_type=F32
    ).astype(BF)
    return (moe_mixed, attn_out.reshape(block_rows, -1))


def pairs_of(lines, move):
    pairs = []
    for line in range(lines):
        for side in range(2):
            for lane in range(2):
                for core in range(2):
                    to = move(line, side, lane, core)
                    pairs.append(
                        (
                            (line * 2 + side) * 4 + lane * 2 + core,
                            (to[0] * 2 + to[1]) * 4 + to[2] * 2 + to[3],
                        )
                    )
    return pairs


def cols(array, start, size):
    return lax.dynamic_slice_in_dim(array, start, size, 1)


def lane_body(
    tokens, expert_ids, route_weights, w_gate, w_up, w_down, query_rows, key_rows, value_rows
):
    seq_index = lax.axis_index("seq")
    expert_index = lax.axis_index("expert")
    lines = lax.axis_size("seq") // 2
    line, side = seq_index // 2, seq_index % 2
    lane, core = expert_index // 2, expert_index % 2
    rows, width = tokens.shape
    quarter = width // 4
    over = 3 * quarter // 4
    hid = w_gate.shape[1]
    experts = lax.axis_size("seq") * EXP_SEQ

    swap_core = pairs_of(lines, lambda l, s, n, c: (l, s, n, 1 - c))
    swap_lane = pairs_of(lines, lambda l, s, n, c: (l, s, 1 - n, c))
    swap_side = pairs_of(lines, lambda l, s, n, c: (l, 1 - s, n, c))
    shift = [
        pairs_of(lines, lambda l, s, n, c, k=k: ((l + k) % lines, s, n, c)) for k in range(lines)
    ]

    def send(value, pairs):
        return lax.ppermute(value, AXES, pairs)

    mine, other = (2 * lane + core) * quarter, (2 * (1 - lane) + core) * quarter
    sib_mine, sib_other = (2 * lane + 1 - core) * quarter, (2 * (1 - lane) + 1 - core) * quarter

    def ordered(weight):
        parts = []
        for near, far in ((mine, other), (sib_mine, sib_other)):
            parts += [
                cols(weight, near, quarter),
                cols(weight, far + over, quarter - over),
                cols(weight, far, over),
            ]
        return jnp.concatenate(parts, axis=1)

    w_in = jnp.concatenate([ordered(w_gate[0]), ordered(w_up[0])], axis=0)
    down = w_down[0]
    down_mine = jnp.concatenate([cols(down, mine, quarter), cols(down, other, quarter)], axis=1)
    down_sib = jnp.concatenate(
        [cols(down, sib_mine, quarter), cols(down, sib_other, quarter)], axis=1
    )
    w_out = jnp.concatenate([down_mine, send(down_sib, swap_core)], axis=0)

    norm_weights = (route_weights / jnp.sum(route_weights, axis=1, keepdims=True)).astype(BF)
    named = expert_ids[:, :, None] == jnp.arange(experts, dtype=jnp.int32)[None, None, :]
    table = jnp.sum(jnp.where(named, norm_weights.astype(F32)[:, :, None], 0.0), axis=1)
    table = table.T.astype(BF)
    key_value = jnp.concatenate([key_rows, value_rows], axis=1)
    small = []
    for k in range(lines):
        head = core * key_rows.shape[1] + ((line + k) % lines) * HD
        packet = jnp.concatenate([cols(key_value, head, HD), table], axis=0)
        small.append(packet if k == 0 else send(packet, shift[k]))
    small = jnp.stack(small)
    small = jnp.stack([small, send(small, swap_side)], axis=1)
    scale = lax.dynamic_index_in_dim(
        small[:, :, rows:], EXP_SEQ * seq_index + lane, 2, keepdims=False
    ).astype(F32)
    own_kv = small[:, :, :rows].reshape(2 * lines * rows, HD)
    sib_kv = send(own_kv, swap_core)
    keys = jnp.where(core == 0, own_kv, sib_kv)
    values = jnp.where(core == 0, sib_kv, own_kv)

    near = jnp.concatenate(
        [cols(tokens, mine, quarter), cols(tokens, other + over, quarter - over)], axis=1
    )
    kept = near.shape[1]
    held = [near] + [send(near, shift[k]) for k in range(1, lines)]
    moe = None
    later = []
    for k in range(lines):
        both = jnp.concatenate([held[k], send(held[k], swap_side)], axis=0)
        crossed = send(both[:, :over], swap_lane)
        half = jnp.concatenate([both, crossed], axis=1)
        full = jnp.concatenate([half, send(half, swap_core)], axis=1)
        gate_up = lax.dot_general(
            full, w_in, (((1,), (1,)), ((), ())), preferred_element_type=F32
        )
        gate_out, up_out = gate_up[:, :hid], gate_up[:, hid:]
        hidden = jax.nn.silu(gate_out) * up_out * scale[k].reshape(2 * rows, 1)
        hidden = hidden.astype(BF)
        hidden = jnp.concatenate([hidden, send(hidden, swap_core)], axis=1)
        part = jnp.dot(hidden, w_out, preferred_element_type=F32)
        crossed = send(part[:, quarter : quarter + over].astype(BF), swap_lane)
        part = jnp.concatenate(
            [
                part[:, :over] + crossed.astype(F32),
                part[:, over:quarter],
                part[:, quarter + over :],
            ],
            axis=1,
        )
        part = part[:rows] + send(part[rows:].astype(BF), swap_side).astype(F32)
        if k == 0:
            moe = part
        else:
            later.append(send(part.astype(BF), shift[lines - k]))
    for part in later:
        moe = moe + part.astype(F32)
    rest = send(moe[:, quarter:].astype(BF), swap_lane).astype(F32)
    moe_mixed = jnp.concatenate([moe[:, :over], moe[:, over:quarter] + rest], axis=1).astype(BF)

    group = query_rows.shape[1] // (2 * lines)
    got = []
    for m in range(2):
        pairs = pairs_of(lines, lambda l, s, n, c: (2 * n + c, (s + m) % 2, l // 2, l % 2))
        piece = cols(query_rows, (2 * expert_index + (side + m) % 2) * group, group)
        got.append(send(piece, pairs))
    same, flipped = got
    queries = jnp.concatenate(
        [jnp.where(side == 0, same, flipped), jnp.where(side == 0, flipped, same)], axis=0
    )
    queries = queries.reshape(2 * rows, group // HD, HD)
    step = jnp.arange(rows, dtype=jnp.int32)
    key_pos = jnp.concatenate(
        [
            (((line - k) % lines) * 2 + (side + m) % 2) * rows + step
            for k in range(lines)
            for m in range(2)
        ]
    )
    query_pos = expert_index * 2 * rows + jnp.arange(2 * rows, dtype=jnp.int32)
    allowed = (key_pos[None, :] <= query_pos[:, None]) & (
        key_pos[None, :] > query_pos[:, None] - BAND
    )
    scores = jnp.einsum("qhd,kd->hqk", queries, keys, preferred_element_type=F32) * HD ** (-0.5)
    scores = jnp.where(allowed[None, :, :], scores, -jnp.inf)
    probs = jax.nn.softmax(scores, axis=-1).astype(BF)
    attn_out = jnp.einsum("hqk,kd->qhd", probs, values, preferred_element_type=F32).astype(BF)
    return (moe_mixed, attn_out.reshape(2 * rows, group))


def solution(mesh):
    placed = (
        P("seq", None),
        P("seq", None),
        P("seq", None),
        P(("seq", "expert"), None, None),
        P(("seq", "expert"), None, None),
        P(("seq", "expert"), None, None),
        P("seq", None),
        P("seq", None),
        P("seq", None),
    )
    fits = mesh.shape["expert"] == 4 and mesh.shape["seq"] == 8
    return jax.shard_map(
        lane_body if fits else general_body,
        mesh=mesh,
        in_specs=placed,
        out_specs=(P("seq", "expert"), P("expert", "seq")),
        check_vma=False,
    )
```

```python
import functools

import jax
import jax.numpy as jnp
from jax import lax
from jax.experimental import pallas as pl
from jax.experimental.pallas import tpu as pltpu
from jax.sharding import PartitionSpec as P

HD = 128
BAND = 1024
EXP_SEQ = 2
AXES = ("seq", "expert")
BF = jnp.bfloat16
F32 = jnp.float32
LIMIT = 56 << 20


def general_body(
    tokens, expert_ids, route_weights, w_gate, w_up, w_down, query_rows, key_rows, value_rows
):
    seq_index = lax.axis_index("seq")
    expert_index = lax.axis_index("expert")
    seq_count = lax.axis_size("seq")
    expert_count = lax.axis_size("expert")
    slice_count = expert_count // EXP_SEQ
    half_index = expert_index // slice_count
    tok_rows, width = tokens.shape
    route_count = expert_ids.shape[1]
    capacity = 3 * tok_rows * route_count // (2 * EXP_SEQ * seq_count)
    norm_weights = (route_weights / jnp.sum(route_weights, axis=1, keepdims=True)).astype(BF)
    targets = jnp.arange(seq_count, dtype=jnp.int32) * EXP_SEQ + half_index
    matched = expert_ids[:, :, None] == targets[None, None, :]
    routed_hit = jnp.sum(matched.astype(F32), axis=1)
    picked = jnp.sum(
        jnp.where(matched, norm_weights.astype(F32)[:, :, None], jnp.float32(0.0)), axis=1
    )
    row_ids = jnp.arange(tok_rows, dtype=jnp.int32)
    earlier = (row_ids[:, None] > row_ids[None, :]).astype(F32)
    slot_rank = jnp.dot(earlier, routed_hit, precision=lax.Precision.HIGHEST)
    slot_ids = jnp.arange(capacity, dtype=F32)
    onehot = (slot_rank.T[:, None, :] == slot_ids[None, :, None]) & (
        routed_hit.T[:, None, :] > 0.5
    )
    selector = onehot.astype(BF)
    outgoing = jnp.einsum("jct,td->jcd", selector, tokens, preferred_element_type=F32).astype(BF)
    incoming = lax.all_to_all(outgoing, "seq", split_axis=0, concat_axis=0, tiled=True)
    slot_count = incoming.shape[1]
    flat_rows = incoming.reshape(-1, width)
    nt = (((1,), (1,)), ((), ()))
    gate_out = lax.dot_general(flat_rows, w_gate[0], nt, preferred_element_type=F32)
    up_out = lax.dot_general(flat_rows, w_up[0], nt, preferred_element_type=F32)
    hidden = (jax.nn.silu(gate_out) * up_out).astype(BF)
    partial_value = jnp.dot(hidden, w_down[0], preferred_element_type=F32).astype(BF)
    partial_value = partial_value.reshape(seq_count, slot_count, width)
    returned = lax.all_to_all(partial_value, "seq", split_axis=0, concat_axis=0, tiled=True)
    combine = (onehot.astype(F32) * picked.T[:, None, :]).astype(BF)
    local_term = jnp.einsum("jct,jcd->td", combine, returned, preferred_element_type=F32)
    moe_mixed = lax.psum_scatter(local_term, "expert", scatter_dimension=1, tiled=True).astype(BF)
    head_total = query_rows.shape[1] // HD
    kv_heads = key_rows.shape[1] // HD
    heads_dev = head_total // seq_count
    block_rows = tok_rows * seq_count // expert_count
    block_start = expert_index * block_rows
    q_all = lax.all_to_all(query_rows, "seq", split_axis=1, concat_axis=0, tiled=True)
    q_block = lax.dynamic_slice_in_dim(q_all, block_start, block_rows, 0).reshape(
        block_rows, heads_dev, HD
    )
    k_full = lax.all_gather(key_rows, "seq", axis=0, tiled=True)
    v_full = lax.all_gather(value_rows, "seq", axis=0, tiled=True)
    kv_head = seq_index * heads_dev // (head_total // kv_heads)
    k_all = lax.dynamic_slice_in_dim(k_full, kv_head * HD, HD, 1)
    v_all = lax.dynamic_slice_in_dim(v_full, kv_head * HD, HD, 1)
    key_pad = jnp.zeros((BAND, HD), BF)
    k_window = lax.dynamic_slice_in_dim(
        jnp.concatenate([key_pad, k_all], axis=0), block_start, BAND + block_rows, 0
    )
    v_window = lax.dynamic_slice_in_dim(
        jnp.concatenate([key_pad, v_all], axis=0), block_start, BAND + block_rows, 0
    )
    query_pos = block_start + jnp.arange(block_rows, dtype=jnp.int32)
    key_pos = block_start - BAND + jnp.arange(BAND + block_rows, dtype=jnp.int32)
    allowed = (
        (key_pos[None, :] <= query_pos[:, None])
        & (key_pos[None, :] > query_pos[:, None] - BAND)
        & (key_pos[None, :] >= 0)
    )
    scores = jnp.einsum("qhd,kd->hqk", q_block, k_window, preferred_element_type=F32) * HD ** (-0.5)
    scores = jnp.where(allowed[None, :, :], scores, -jnp.inf)
    attn_probs = jax.nn.softmax(scores, axis=-1).astype(BF)
    attn_out = jnp.einsum(
        "hqk,kd->qhd", attn_probs, v_window, preferred_element_type=F32
    ).astype(BF)
    return (moe_mixed, attn_out.reshape(block_rows, -1))


def pairs_of(lines, move):
    pairs = []
    for line in range(lines):
        for side in range(2):
            for lane in range(2):
                for core in range(2):
                    to = move(line, side, lane, core)
                    pairs.append(
                        (
                            (line * 2 + side) * 4 + lane * 2 + core,
                            (to[0] * 2 + to[1]) * 4 + to[2] * 2 + to[3],
                        )
                    )
    return pairs


def cols(array, start, size):
    return lax.dynamic_slice_in_dim(array, start, size, 1)


VMEM = pl.BlockSpec(memory_space=pltpu.VMEM)
HBM = pl.BlockSpec(memory_space=pltpu.HBM)
LIGHT = pl.CostEstimate(flops=0, bytes_accessed=1, transcendentals=0)
NT = (((1,), (1,)), ((), ()))
TABLE = 128


def block_of(number, size):
    return pl.ds(pl.multiple_of(number * size, size), size)


def place_here():
    place = lax.axis_index("expert")
    return place // 2, lax.rem(place, 2)


def slices_kernel(tokens, ids, weights, near, far):
    lane, core = place_here()
    rows, size = far.shape
    here = block_of(core, rows)
    near[:, :size] = tokens[here, block_of(lane, size)]
    far[...] = tokens[here, block_of(1 - lane, size)]
    raw = weights[...]
    norm = (raw / jnp.sum(raw, axis=0, keepdims=True)).astype(BF).astype(F32)
    experts = 16 * ((EXP_SEQ * lax.axis_size("seq") + 15) // 16)
    number = lax.broadcasted_iota(jnp.int32, (experts, 2 * rows), 0)
    table = jnp.zeros((experts, 2 * rows), F32)
    for a in range(ids.shape[0]):
        table += jnp.where(number == ids[a : a + 1], norm[a : a + 1], 0.0)
    table = jnp.concatenate([table, jnp.zeros((TABLE - experts, 2 * rows), F32)], axis=0).T
    near[:, size:] = jnp.where(core == 0, table[:rows], table[rows:]).astype(BF)


def slices_of(tokens, ids, weights):
    rows, width = tokens.shape
    return pl.pallas_call(
        slices_kernel,
        cost_estimate=LIGHT,
        out_shape=(
            jax.ShapeDtypeStruct((rows // 2, width // 2 + TABLE), BF),
            jax.ShapeDtypeStruct((rows // 2, width // 2), BF),
        ),
        in_specs=[VMEM] * 3,
        out_specs=(VMEM,) * 2,
    )(tokens, ids.T, weights.T)


def expert_kernel(count, *refs):
    near, far, opp_near, opp_far = (refs[i * count : (i + 1) * count] for i in range(4))
    weights = refs[4 * count : 4 * count + 6]
    opp_far_out, own_far_out, opp_out, own_out, rows_in, held, sems = refs[4 * count + 6 :]
    lane, _ = place_here()
    rows, size = far[0].shape[0], held.shape[2] // 2
    expert = EXP_SEQ * lax.axis_index("seq") + lane
    hid = held.shape[1] // 2
    copies = []
    for n, weight in enumerate(weights):
        copies.append(
            pltpu.make_async_copy(
                weight.at[0], held.at[n // 2, pl.ds(n % 2 * hid, hid)], sems.at[n]
            )
        )
    for copy in copies:
        copy.start()
    for column, pieces in ((lane, near + opp_near), (1 - lane, far + opp_far)):
        for number, piece in enumerate(pieces):
            at = slice(number * rows, (number + 1) * rows)
            rows_in[at, block_of(column, size)] = piece[:, :size]
    number = lax.broadcasted_iota(jnp.int32, (rows, TABLE), 1)
    scale = jnp.concatenate(
        [
            jnp.sum(
                jnp.where(number == expert, piece[:, size:].astype(F32), 0.0),
                axis=1,
                keepdims=True,
            )
            for piece in near + opp_near
        ],
        axis=0,
    )
    hidden = []
    for p in range(2):
        copies[2 * p].wait()
        copies[2 * p + 1].wait()
        value = lax.dot_general(rows_in[...], held[p], NT, preferred_element_type=F32)
        gate, up = value[:, :hid], value[:, hid:]
        hidden.append((gate * (0.5 + 0.5 * jnp.tanh(0.5 * gate)) * up * scale).astype(BF))
    hidden = jnp.concatenate(hidden, axis=1)
    copies[4].wait()
    copies[5].wait()
    many = count * rows
    for column in (1 - lane, lane):
        value = jnp.dot(hidden, held[2, :, block_of(column, size)], preferred_element_type=F32)
        if column is lane:
            own_out[...] = value[:many]
            opp_out[...] = value[many:]
        else:
            own_far_out[...] = value[:many].astype(BF)
            opp_far_out[...] = value[many:].astype(BF)


def expert_terms(near, far, opp_near, opp_far, *weights):
    count = len(near)
    rows = near[0].shape[0]
    hid, width = weights[0].shape[1:]
    shape = (count * rows, width // 2)
    return pl.pallas_call(
        functools.partial(expert_kernel, count),
        cost_estimate=LIGHT,
        out_shape=tuple(jax.ShapeDtypeStruct(shape, kind) for kind in (BF, BF, F32, F32)),
        in_specs=[VMEM] * (4 * count) + [HBM] * 6,
        out_specs=(VMEM,) * 4,
        scratch_shapes=[
            pltpu.VMEM((2 * count * rows, width), BF),
            pltpu.VMEM((3, 2 * hid, width), BF),
            pltpu.SemaphoreType.DMA((6,)),
        ],
        compiler_params=pltpu.CompilerParams(vmem_limit_bytes=LIMIT),
    )(*near, *far, *opp_near, *opp_far, *weights)


def pack_kernel(keys, values, *packets):
    line = lax.axis_index("seq") // 2
    _, core = place_here()
    for k, packet in enumerate(packets):
        head = block_of(lax.rem(line + k, len(packets)), HD)
        packet[...] = jnp.where(core == 0, keys[:, head], values[:, head])


def packed(keys, values, lines):
    return pl.pallas_call(
        pack_kernel,
        cost_estimate=LIGHT,
        out_shape=(jax.ShapeDtypeStruct((keys.shape[0], HD), BF),) * lines,
        in_specs=[VMEM] * 2,
        out_specs=(VMEM,) * lines,
    )(keys, values)


def attend_kernel(query_a, query_b, own, sib, out, bias):
    rows = query_a.shape[0]
    blocks = own.shape[0] // rows
    line, side = lax.axis_index("seq") // 2, lax.rem(lax.axis_index("seq"), 2)
    _, core = place_here()
    keys = jnp.where(core == 0, own[...], sib[...])
    values = jnp.where(core == 0, sib[...], own[...])
    down = lax.broadcasted_iota(jnp.int32, (rows, rows), 0)
    along = lax.broadcasted_iota(jnp.int32, (rows, rows), 1)
    for number, query in enumerate((query_a, query_b)):
        upper = lax.rem(side + number, 2)
        at = 2 * lax.axis_index("expert") + upper
        for b in range(blocks):
            k, m = b // 2, b % 2
            behind = 2 * lax.rem(line + blocks // 2 - k, blocks // 2) + lax.rem(side + m, 2)
            behind = (at - behind) * rows + down - along
            bias[:, b * rows : (b + 1) * rows] = jnp.where(
                (behind >= 0) & (behind < BAND), 0.0, -1e30
            )
        target = block_of(upper, rows)
        for h in range(query.shape[1] // HD):
            head = slice(h * HD, (h + 1) * HD)
            scores = lax.dot_general(
                query[:, head], keys, (((1,), (1,)), ((), ())), preferred_element_type=F32
            )
            scores = scores * HD ** (-0.5) + bias[...]
            probs = jnp.exp(scores - jnp.max(scores, axis=1, keepdims=True))
            total = jnp.sum(probs, axis=1, keepdims=True)
            mixed = jnp.dot(probs.astype(BF), values, preferred_element_type=F32)
            out[target, head] = (mixed / total).astype(BF)


def attended(query_a, query_b, own, sib):
    rows, width = query_a.shape
    count = own.shape[0]
    return pl.pallas_call(
        attend_kernel,
        cost_estimate=LIGHT,
        out_shape=jax.ShapeDtypeStruct((2 * rows, width), BF),
        in_specs=[VMEM] * 4,
        out_specs=VMEM,
        scratch_shapes=[pltpu.VMEM((rows, count), F32)],
        compiler_params=pltpu.CompilerParams(vmem_limit_bytes=24 << 20),
    )(query_a, query_b, own, sib)


def lane_body(
    tokens, expert_ids, route_weights, w_gate, w_up, w_down, query_rows, key_rows, value_rows
):
    seq_index = lax.axis_index("seq")
    expert_index = lax.axis_index("expert")
    lines = lax.axis_size("seq") // 2
    side = seq_index % 2
    lane, core = expert_index // 2, expert_index % 2
    rows, width = tokens.shape
    quarter = width // 4
    group = query_rows.shape[1] // (2 * lines)

    routes = {
        "core": pairs_of(lines, lambda l, s, n, c: (l, s, n, 1 - c)),
        "lane": pairs_of(lines, lambda l, s, n, c: (l, s, 1 - n, c)),
    }
    for k in range(lines):
        for m in range(2):
            routes[k, m] = pairs_of(
                lines, lambda l, s, n, c: ((l + k) % lines, (s + m) % 2, n, c)
            )
            routes["query", m] = pairs_of(
                lines, lambda l, s, n, c: (2 * c + n, (s + m) % 2, l // 2, l % 2)
            )
    flight = {}
    now = [jnp.zeros((), F32)]

    def at(value):
        value, now[0] = lax.optimization_barrier((value, now[0]))
        return value

    def start(name, value, route):
        with jax.named_scope("send_" + name):
            flight[name] = lax.ppermute(at(value), AXES, routes[route])

    def done(name):
        return at(flight.pop(name))

    near, far, opp_near, opp_far, parts, moe = {}, {}, {}, {}, {}, {}
    half = rows // 2

    def line_done(k, to=None):
        near[k] = done(f"zn{k}")
        if to:
            start(f"zn{to}", near[k], (1, 0))

    def side_start(k):
        start(f"y{k}", near[k], (0, 1))

    def side_done(k):
        opp_near[k] = done(f"y{k}")
        start(f"x{k}", opp_near[k], "lane")

    def lane_done(k):
        opp_far[k] = done(f"x{k}")

    def expert_on(g):
        pieces = [[part[k] for k in g] for part in (near, far, opp_near, opp_far)]
        parts[g] = at(expert_terms(*pieces, w_gate, w_up, wg, wu, w_down, wd))

    def to_lane(g):
        start(f"rx{g[0]}", parts[g][0], "lane")
        start(f"rw{g[0]}", parts[g][1], "lane")

    def to_side(g):
        summed = (parts[g][2] + done(f"rx{g[0]}").astype(F32)).astype(BF)
        start(f"ry{g[0]}", summed, (0, 1))

    def sums_of(g):
        total = parts[g][3] + done(f"rw{g[0]}").astype(F32) + done(f"ry{g[0]}").astype(F32)
        for number, k in enumerate(g):
            moe[k] = total[number * half : (number + 1) * half]
            if k:
                moe[k] = moe[k].astype(BF)

    group_a, group_b = (0, 1), (2, 3)
    near[0], far[0] = at(slices_of(tokens, expert_ids, route_weights))
    start("zn1", near[0], (1, 0))
    side_start(0)
    start("zn3", near[0], (3, 0))
    start("wg", w_gate, "core")
    start("wu", w_up, "core")
    line_done(1, 2)
    wg = done("wg")
    side_done(0)
    wu = done("wu")
    side_start(1)
    line_done(3)
    start("zf3", far[0], (3, 0))
    start("wd", w_down, "core")
    lane_done(0)
    side_done(1)
    line_done(2)
    side_start(2)
    far[3] = done("zf3")
    start("zf1", far[0], (1, 0))
    side_start(3)
    wd = done("wd")
    start("yf3", far[3], (0, 1))
    lane_done(1)
    far[1] = done("zf1")
    start("zf2", far[1], (1, 0))
    side_done(2)
    packets = list(at(packed(key_rows, value_rows, lines)))
    start("kz1", packets[1], (1, 0))
    expert_on(group_a)
    to_lane(group_a)
    opp_near[3] = done("y3")
    opp_far[3] = done("yf3")
    lane_done(2)
    far[2] = done("zf2")
    packets[1] = done("kz1")
    start("kz2", packets[2], (2, 0))
    start("kz3", packets[3], (3, 0))
    for m in range(2):
        block = 2 * (2 * core + lane) + (side + m) % 2
        packets.append(cols(query_rows, block * group, group))
    start("q0", packets[lines], ("query", 0))
    expert_on(group_b)
    packets[2] = done("kz2")
    packets[3] = done("kz3")
    small = at(jnp.stack(packets[:lines]))
    to_lane(group_b)
    query_a = done("q0")
    to_side(group_a)
    start("ky", small, (0, 1))
    parts[group_a] = parts[group_a][:2] + (done("rw0"), parts[group_a][3])
    start("q1", packets[lines + 1], ("query", 1))
    small = jnp.stack([small, done("ky")], axis=1)
    to_side(group_b)
    own_kv = small.reshape(2 * lines * rows, HD)
    start("kc", own_kv, "core")
    total = parts[group_a][3] + parts[group_a][2].astype(F32) + done("ry0").astype(F32)
    moe[0], moe[1] = total[:half], total[half:].astype(BF)
    start("rz1", moe[1], (3, 0))
    sib_kv = done("kc")
    query_b = done("q1")
    attn_out = at(attended(query_a, query_b, own_kv, sib_kv))
    rz1 = done("rz1")
    sums_of(group_b)
    start("rz2", moe[2], (2, 0))
    start("rz3", moe[3], (1, 0))
    total = moe[0] + rz1.astype(F32)
    total = total + done("rz3").astype(F32)
    total = (total + done("rz2").astype(F32)).astype(BF)
    kept, passed = (cols(total, c * quarter, quarter) for c in (core, 1 - core))
    start("last", passed, "core")
    passed = done("last")
    moe_mixed = jnp.concatenate(
        [jnp.where(core == 0, kept, passed), jnp.where(core == 0, passed, kept)], axis=0
    )
    return (moe_mixed + now[0].astype(BF), attn_out)


def solution(mesh):
    placed = (
        P("seq", None),
        P("seq", None),
        P("seq", None),
        P(("seq", "expert"), None, None),
        P(("seq", "expert"), None, None),
        P(("seq", "expert"), None, None),
        P("seq", None),
        P("seq", None),
        P("seq", None),
    )
    fits = mesh.shape["expert"] == 4 and mesh.shape["seq"] == 8
    return jax.shard_map(
        lane_body if fits else general_body,
        mesh=mesh,
        in_specs=placed,
        out_specs=(P("seq", "expert"), P("expert", "seq")),
        check_vma=False,
    )
```

```python
import functools

import jax
import jax.numpy as jnp
from jax import lax
from jax.experimental import pallas as pl
from jax.experimental.pallas import tpu as pltpu
from jax.sharding import PartitionSpec as P

HD = 128
BAND = 1024
EXP_SEQ = 2
AXES = ("seq", "expert")
BF = jnp.bfloat16
F32 = jnp.float32
LIMIT = 56 << 20


def general_body(
    tokens, expert_ids, route_weights, w_gate, w_up, w_down, query_rows, key_rows, value_rows
):
    seq_index = lax.axis_index("seq")
    expert_index = lax.axis_index("expert")
    seq_count = lax.axis_size("seq")
    expert_count = lax.axis_size("expert")
    slice_count = expert_count // EXP_SEQ
    half_index = expert_index // slice_count
    tok_rows, width = tokens.shape
    route_count = expert_ids.shape[1]
    capacity = 3 * tok_rows * route_count // (2 * EXP_SEQ * seq_count)
    norm_weights = (route_weights / jnp.sum(route_weights, axis=1, keepdims=True)).astype(BF)
    targets = jnp.arange(seq_count, dtype=jnp.int32) * EXP_SEQ + half_index
    matched = expert_ids[:, :, None] == targets[None, None, :]
    routed_hit = jnp.sum(matched.astype(F32), axis=1)
    picked = jnp.sum(
        jnp.where(matched, norm_weights.astype(F32)[:, :, None], jnp.float32(0.0)), axis=1
    )
    row_ids = jnp.arange(tok_rows, dtype=jnp.int32)
    earlier = (row_ids[:, None] > row_ids[None, :]).astype(F32)
    slot_rank = jnp.dot(earlier, routed_hit, precision=lax.Precision.HIGHEST)
    slot_ids = jnp.arange(capacity, dtype=F32)
    onehot = (slot_rank.T[:, None, :] == slot_ids[None, :, None]) & (
        routed_hit.T[:, None, :] > 0.5
    )
    selector = onehot.astype(BF)
    outgoing = jnp.einsum("jct,td->jcd", selector, tokens, preferred_element_type=F32).astype(BF)
    incoming = lax.all_to_all(outgoing, "seq", split_axis=0, concat_axis=0, tiled=True)
    slot_count = incoming.shape[1]
    flat_rows = incoming.reshape(-1, width)
    nt = (((1,), (1,)), ((), ()))
    gate_out = lax.dot_general(flat_rows, w_gate[0], nt, preferred_element_type=F32)
    up_out = lax.dot_general(flat_rows, w_up[0], nt, preferred_element_type=F32)
    hidden = (jax.nn.silu(gate_out) * up_out).astype(BF)
    partial_value = jnp.dot(hidden, w_down[0], preferred_element_type=F32).astype(BF)
    partial_value = partial_value.reshape(seq_count, slot_count, width)
    returned = lax.all_to_all(partial_value, "seq", split_axis=0, concat_axis=0, tiled=True)
    combine = (onehot.astype(F32) * picked.T[:, None, :]).astype(BF)
    local_term = jnp.einsum("jct,jcd->td", combine, returned, preferred_element_type=F32)
    moe_mixed = lax.psum_scatter(local_term, "expert", scatter_dimension=1, tiled=True).astype(BF)
    head_total = query_rows.shape[1] // HD
    kv_heads = key_rows.shape[1] // HD
    heads_dev = head_total // seq_count
    block_rows = tok_rows * seq_count // expert_count
    block_start = expert_index * block_rows
    q_all = lax.all_to_all(query_rows, "seq", split_axis=1, concat_axis=0, tiled=True)
    q_block = lax.dynamic_slice_in_dim(q_all, block_start, block_rows, 0).reshape(
        block_rows, heads_dev, HD
    )
    k_full = lax.all_gather(key_rows, "seq", axis=0, tiled=True)
    v_full = lax.all_gather(value_rows, "seq", axis=0, tiled=True)
    kv_head = seq_index * heads_dev // (head_total // kv_heads)
    k_all = lax.dynamic_slice_in_dim(k_full, kv_head * HD, HD, 1)
    v_all = lax.dynamic_slice_in_dim(v_full, kv_head * HD, HD, 1)
    key_pad = jnp.zeros((BAND, HD), BF)
    k_window = lax.dynamic_slice_in_dim(
        jnp.concatenate([key_pad, k_all], axis=0), block_start, BAND + block_rows, 0
    )
    v_window = lax.dynamic_slice_in_dim(
        jnp.concatenate([key_pad, v_all], axis=0), block_start, BAND + block_rows, 0
    )
    query_pos = block_start + jnp.arange(block_rows, dtype=jnp.int32)
    key_pos = block_start - BAND + jnp.arange(BAND + block_rows, dtype=jnp.int32)
    allowed = (
        (key_pos[None, :] <= query_pos[:, None])
        & (key_pos[None, :] > query_pos[:, None] - BAND)
        & (key_pos[None, :] >= 0)
    )
    scores = jnp.einsum("qhd,kd->hqk", q_block, k_window, preferred_element_type=F32) * HD ** (-0.5)
    scores = jnp.where(allowed[None, :, :], scores, -jnp.inf)
    attn_probs = jax.nn.softmax(scores, axis=-1).astype(BF)
    attn_out = jnp.einsum(
        "hqk,kd->qhd", attn_probs, v_window, preferred_element_type=F32
    ).astype(BF)
    return (moe_mixed, attn_out.reshape(block_rows, -1))


def pairs_of(lines, move):
    pairs = []
    for line in range(lines):
        for side in range(2):
            for lane in range(2):
                for core in range(2):
                    to = move(line, side, lane, core)
                    pairs.append(
                        (
                            (line * 2 + side) * 4 + lane * 2 + core,
                            (to[0] * 2 + to[1]) * 4 + to[2] * 2 + to[3],
                        )
                    )
    return pairs


def cols(array, start, size):
    return lax.dynamic_slice_in_dim(array, start, size, 1)


VMEM = pl.BlockSpec(memory_space=pltpu.VMEM)
HBM = pl.BlockSpec(memory_space=pltpu.HBM)
LIGHT = pl.CostEstimate(flops=0, bytes_accessed=1, transcendentals=0)
NT = (((1,), (1,)), ((), ()))
TABLE = 128
CHUNK = 384
AHEAD = 6


def block_of(number, size):
    return pl.ds(pl.multiple_of(number * size, size), size)


def place_here():
    place = lax.axis_index("expert")
    return place // 2, lax.rem(place, 2)


def rows_kernel(tokens, ids, weights, out):
    _, core = place_here()
    rows, width = out.shape[0], tokens.shape[1]
    out[:, :width] = tokens[block_of(core, rows), :]
    raw = weights[...]
    norm = (raw / jnp.sum(raw, axis=0, keepdims=True)).astype(BF).astype(F32)
    experts = 16 * ((EXP_SEQ * lax.axis_size("seq") + 15) // 16)
    number = lax.broadcasted_iota(jnp.int32, (experts, 2 * rows), 0)
    table = jnp.zeros((experts, 2 * rows), F32)
    for a in range(ids.shape[0]):
        table += jnp.where(number == ids[a : a + 1], norm[a : a + 1], 0.0)
    table = jnp.concatenate([table, jnp.zeros((TABLE - experts, 2 * rows), F32)], axis=0).T
    out[:, width:] = jnp.where(core == 0, table[:rows], table[rows:]).astype(BF)


def rows_of(tokens, ids, weights):
    rows, width = tokens.shape
    return pl.pallas_call(
        rows_kernel,
        cost_estimate=LIGHT,
        out_shape=jax.ShapeDtypeStruct((rows // 2, width + TABLE), BF),
        in_specs=[VMEM] * 3,
        out_specs=VMEM,
    )(tokens, ids.T, weights.T)


def expert_kernel(count, *refs):
    pieces, refs = refs[:count], refs[count:]
    gate_up, down = refs[:4], refs[4:6]
    opp_far_out, own_far_out, opp_out, own_out, rows_in, hidden = refs[6:]
    lane, _ = place_here()
    hid, width = gate_up[0].shape[1:]
    rows, size = pieces[0].shape[0], width // 2
    expert = EXP_SEQ * lax.axis_index("seq") + lane
    for number, piece in enumerate(pieces):
        rows_in[number * rows : (number + 1) * rows] = piece[:, :width]
    number = lax.broadcasted_iota(jnp.int32, (rows, TABLE), 1)
    scale = jnp.concatenate(
        [
            jnp.sum(
                jnp.where(number == expert, piece[:, width:].astype(F32), 0.0),
                axis=1,
                keepdims=True,
            )
            for piece in pieces
        ],
        axis=0,
    )
    for n in range(2):
        gate, up = (
            lax.dot_general(rows_in[...], gate_up[2 * n + i][0], NT, preferred_element_type=F32)
            for i in range(2)
        )
        hidden[:, n * hid : (n + 1) * hid] = (
            gate * (0.5 + 0.5 * jnp.tanh(0.5 * gate)) * up * scale
        ).astype(BF)
    many = count * rows // 2
    for column in (1 - lane, lane):
        value = 0.0
        for n in range(2):
            value += jnp.dot(
                hidden[:, n * hid : (n + 1) * hid],
                down[n][0, :, block_of(column, size)],
                preferred_element_type=F32,
            )
        if column is lane:
            own_out[...] = value[:many]
            opp_out[...] = value[many:]
        else:
            own_far_out[...] = value[:many].astype(BF)
            opp_far_out[...] = value[many:].astype(BF)


def expert_terms(pieces, *weights):
    count = len(pieces)
    rows = pieces[0].shape[0]
    hid, width = weights[0].shape[1:]
    shape = (count * rows // 2, width // 2)
    return pl.pallas_call(
        functools.partial(expert_kernel, count),
        cost_estimate=LIGHT,
        out_shape=tuple(jax.ShapeDtypeStruct(shape, kind) for kind in (BF, BF, F32, F32)),
        in_specs=[VMEM] * (count + 6),
        out_specs=(VMEM,) * 4,
        scratch_shapes=[
            pltpu.VMEM((count * rows, width), BF),
            pltpu.VMEM((count * rows, 2 * hid), BF),
        ],
        compiler_params=pltpu.CompilerParams(vmem_limit_bytes=32 << 20),
    )(*pieces, *weights)


def pack_kernel(keys, values, queries, *refs):
    packets, pieces, sems = refs[:-3], refs[-3:-1], refs[-1]
    line, side = lax.axis_index("seq") // 2, lax.rem(lax.axis_index("seq"), 2)
    lane, core = place_here()
    size = pieces[0].shape[1]
    copies = []
    for m, piece in enumerate(pieces):
        block = 2 * (2 * core + lane) + lax.rem(side + m, 2)
        copies.append(
            pltpu.make_async_copy(queries.at[:, block_of(block, size)], piece, sems.at[m])
        )
    for copy in copies:
        copy.start()
    for k, packet in enumerate(packets):
        head = block_of(lax.rem(line + k, len(packets)), HD)
        packet[:, :HD] = keys[:, head]
        packet[:, HD:] = values[:, head]
    for copy in copies:
        copy.wait()


def packed(keys, values, queries, lines):
    rows = keys.shape[0]
    packet = jax.ShapeDtypeStruct((rows, 2 * HD), BF)
    piece = jax.ShapeDtypeStruct((rows, queries.shape[1] // (2 * lines)), BF)
    return pl.pallas_call(
        pack_kernel,
        cost_estimate=LIGHT,
        out_shape=(packet,) * lines + (piece,) * 2,
        in_specs=[VMEM] * 2 + [HBM],
        out_specs=(VMEM,) * (lines + 2),
        scratch_shapes=[pltpu.SemaphoreType.DMA((2,))],
    )(keys, values, queries)


def attend_kernel(query_a, query_b, key_value, out, bias):
    rows = query_a.shape[0]
    blocks = key_value.shape[0] // rows
    line, side = lax.axis_index("seq") // 2, lax.rem(lax.axis_index("seq"), 2)
    keys, values = key_value[:, :HD], key_value[:, HD:]
    down = lax.broadcasted_iota(jnp.int32, (rows, rows), 0)
    along = lax.broadcasted_iota(jnp.int32, (rows, rows), 1)
    for number, query in enumerate((query_a, query_b)):
        upper = lax.rem(side + number, 2)
        at = 2 * lax.axis_index("expert") + upper
        for b in range(blocks):
            k, m = b // 2, b % 2
            behind = 2 * lax.rem(line + blocks // 2 - k, blocks // 2) + lax.rem(side + m, 2)
            behind = (at - behind) * rows + down - along
            bias[:, b * rows : (b + 1) * rows] = jnp.where(
                (behind >= 0) & (behind < BAND), 0.0, -1e30
            )
        target = block_of(upper, rows)
        for h in range(query.shape[1] // HD):
            head = slice(h * HD, (h + 1) * HD)
            scores = lax.dot_general(
                query[:, head], keys, (((1,), (1,)), ((), ())), preferred_element_type=F32
            )
            scores = scores * HD ** (-0.5) + bias[...]
            probs = jnp.exp(scores - jnp.max(scores, axis=1, keepdims=True))
            total = jnp.sum(probs, axis=1, keepdims=True)
            mixed = jnp.dot(probs.astype(BF), values, preferred_element_type=F32)
            out[target, head] = (mixed / total).astype(BF)


def attended(query_a, query_b, key_value):
    rows, width = query_a.shape
    count = key_value.shape[0]
    return pl.pallas_call(
        attend_kernel,
        cost_estimate=LIGHT,
        out_shape=jax.ShapeDtypeStruct((2 * rows, width), BF),
        in_specs=[VMEM] * 3,
        out_specs=VMEM,
        scratch_shapes=[pltpu.VMEM((rows, count), F32)],
        compiler_params=pltpu.CompilerParams(vmem_limit_bytes=24 << 20),
    )(query_a, query_b, key_value)


def lane_body(
    tokens, expert_ids, route_weights, w_gate, w_up, w_down, query_rows, key_rows, value_rows
):
    seq_index = lax.axis_index("seq")
    expert_index = lax.axis_index("expert")
    lines = lax.axis_size("seq") // 2
    side = seq_index % 2
    lane, core = expert_index // 2, expert_index % 2
    rows, width = tokens.shape
    quarter = width // 4

    routes = {
        "core": pairs_of(lines, lambda l, s, n, c: (l, s, n, 1 - c)),
        "lane": pairs_of(lines, lambda l, s, n, c: (l, s, 1 - n, c)),
    }
    for k in range(lines):
        for m in range(2):
            routes[k, m] = pairs_of(
                lines, lambda l, s, n, c: ((l + k) % lines, (s + m) % 2, n, c)
            )
            routes["query", m] = pairs_of(
                lines, lambda l, s, n, c: (2 * c + n, (s + m) % 2, l // 2, l % 2)
            )
    flight = {}
    now = [jnp.zeros((), F32)]

    def at(value):
        value, now[0] = lax.optimization_barrier((value, now[0]))
        return value

    def start(name, value, route):
        with jax.named_scope("send_" + name):
            flight[name] = lax.ppermute(at(value), AXES, routes[route])

    def done(name):
        return at(flight.pop(name))

    own, opp, parts, moe = {}, {}, {}, {}
    half = rows // 2

    def expert_on(k):
        parts[k] = at(expert_terms([own[k], opp[k]], w_gate, w_up, wg, wu, w_down, wd))

    def to_side(k):
        summed = parts[k][2] + done(f"rx{k}").astype(F32)
        start(f"ry{k}", summed.astype(BF), (0, 1))

    def lane_start(k):
        start(f"rw{k}", parts[k][1], "lane")

    def lane_done(k):
        moe[k] = moe.get(k, parts[k][3]) + done(f"rw{k}").astype(F32)

    def side_done(k):
        moe[k] = moe.get(k, parts[k][3]) + done(f"ry{k}").astype(F32)

    own[0] = at(rows_of(tokens, expert_ids, route_weights))
    start("z1", own[0], (1, 0))
    start("y0", own[0], (0, 1))
    start("wg", w_gate, "core")
    start("wu", w_up, "core")
    *packets, query_a, query_b = at(packed(key_rows, value_rows, query_rows, lines))
    start("kz1", packets[1], (1, 0))
    packets[1] = done("kz1")
    own[1] = done("z1")
    opp[0] = done("y0")
    wg = done("wg")
    wu = done("wu")
    start("z2", own[1], (1, 0))
    start("y1", own[1], (0, 1))
    start("wd", w_down, "core")
    start("q0", query_a, ("query", 0))
    wd = done("wd")
    expert_on(0)
    opp[1] = done("y1")
    own[2] = done("z2")
    query_a = done("q0")
    start("y2", own[2], (0, 1))
    start("z3", own[0], (3, 0))
    start("rx0", parts[0][0], "lane")
    for k in (2, 3):
        start(f"kz{k}", packets[k], (k, 0))
    expert_on(1)
    opp[2] = done("y2")
    own[3] = done("z3")
    for k in (2, 3):
        packets[k] = done(f"kz{k}")
    small = at(jnp.stack(packets))
    to_side(0)
    start("y3", own[3], (0, 1))
    start("rx1", parts[1][0], "lane")
    lane_start(1)
    start("q1", query_b, ("query", 1))
    expert_on(2)
    opp[3] = done("y3")
    start("rx2", parts[2][0], "lane")
    expert_on(3)
    side_done(0)
    lane_done(1)
    start("rx3", parts[3][0], "lane")
    to_side(1)
    to_side(2)
    lane_start(2)
    query_b = done("q1")
    start("ky", small, (0, 1))
    to_side(3)
    lane_start(3)
    side_done(1)
    start("rz1", moe[1].astype(BF), (3, 0))
    side_done(2)
    lane_done(2)
    start("rz2", moe[2].astype(BF), (1, 0))
    key_value = jnp.stack([small, done("ky")], axis=1).reshape(2 * lines * rows, 2 * HD)
    side_done(3)
    lane_done(3)
    lane_start(0)
    block = (moe[3] + done("rz2").astype(F32)).astype(BF)
    start("rz3", block, (1, 0))
    attn_out = at(attended(query_a, query_b, key_value))
    lane_done(0)
    total = moe[0] + done("rz1").astype(F32)
    total = (total + done("rz3").astype(F32)).astype(BF)
    kept, passed = (cols(total, c * quarter, quarter) for c in (core, 1 - core))
    start("last", passed, "core")
    passed = done("last")
    moe_mixed = jnp.concatenate(
        [jnp.where(core == 0, kept, passed), jnp.where(core == 0, passed, kept)], axis=0
    )
    return (moe_mixed + now[0].astype(BF), attn_out)


def solution(mesh):
    placed = (
        P("seq", None),
        P("seq", None),
        P("seq", None),
        P(("seq", "expert"), None, None),
        P(("seq", "expert"), None, None),
        P(("seq", "expert"), None, None),
        P("seq", None),
        P("seq", None),
        P("seq", None),
    )
    fits = mesh.shape["expert"] == 4 and mesh.shape["seq"] == 8
    return jax.shard_map(
        lane_body if fits else general_body,
        mesh=mesh,
        in_specs=placed,
        out_specs=(P("seq", "expert"), P("expert", "seq")),
        check_vma=False,
    )
```

```python
import functools

import jax
import jax.numpy as jnp
from jax import lax
from jax.experimental import pallas as pl
from jax.experimental.pallas import tpu as pltpu
from jax.sharding import PartitionSpec as P

HD = 128
BAND = 1024
EXP_SEQ = 2
AXES = ("seq", "expert")
BF = jnp.bfloat16
F32 = jnp.float32
LIMIT = 56 << 20


def general_body(
    tokens, expert_ids, route_weights, w_gate, w_up, w_down, query_rows, key_rows, value_rows
):
    seq_index = lax.axis_index("seq")
    expert_index = lax.axis_index("expert")
    seq_count = lax.axis_size("seq")
    expert_count = lax.axis_size("expert")
    slice_count = expert_count // EXP_SEQ
    half_index = expert_index // slice_count
    tok_rows, width = tokens.shape
    route_count = expert_ids.shape[1]
    capacity = 3 * tok_rows * route_count // (2 * EXP_SEQ * seq_count)
    norm_weights = (route_weights / jnp.sum(route_weights, axis=1, keepdims=True)).astype(BF)
    targets = jnp.arange(seq_count, dtype=jnp.int32) * EXP_SEQ + half_index
    matched = expert_ids[:, :, None] == targets[None, None, :]
    routed_hit = jnp.sum(matched.astype(F32), axis=1)
    picked = jnp.sum(
        jnp.where(matched, norm_weights.astype(F32)[:, :, None], jnp.float32(0.0)), axis=1
    )
    row_ids = jnp.arange(tok_rows, dtype=jnp.int32)
    earlier = (row_ids[:, None] > row_ids[None, :]).astype(F32)
    slot_rank = jnp.dot(earlier, routed_hit, precision=lax.Precision.HIGHEST)
    slot_ids = jnp.arange(capacity, dtype=F32)
    onehot = (slot_rank.T[:, None, :] == slot_ids[None, :, None]) & (
        routed_hit.T[:, None, :] > 0.5
    )
    selector = onehot.astype(BF)
    outgoing = jnp.einsum("jct,td->jcd", selector, tokens, preferred_element_type=F32).astype(BF)
    incoming = lax.all_to_all(outgoing, "seq", split_axis=0, concat_axis=0, tiled=True)
    slot_count = incoming.shape[1]
    flat_rows = incoming.reshape(-1, width)
    nt = (((1,), (1,)), ((), ()))
    gate_out = lax.dot_general(flat_rows, w_gate[0], nt, preferred_element_type=F32)
    up_out = lax.dot_general(flat_rows, w_up[0], nt, preferred_element_type=F32)
    hidden = (jax.nn.silu(gate_out) * up_out).astype(BF)
    partial_value = jnp.dot(hidden, w_down[0], preferred_element_type=F32).astype(BF)
    partial_value = partial_value.reshape(seq_count, slot_count, width)
    returned = lax.all_to_all(partial_value, "seq", split_axis=0, concat_axis=0, tiled=True)
    combine = (onehot.astype(F32) * picked.T[:, None, :]).astype(BF)
    local_term = jnp.einsum("jct,jcd->td", combine, returned, preferred_element_type=F32)
    moe_mixed = lax.psum_scatter(local_term, "expert", scatter_dimension=1, tiled=True).astype(BF)
    head_total = query_rows.shape[1] // HD
    kv_heads = key_rows.shape[1] // HD
    heads_dev = head_total // seq_count
    block_rows = tok_rows * seq_count // expert_count
    block_start = expert_index * block_rows
    q_all = lax.all_to_all(query_rows, "seq", split_axis=1, concat_axis=0, tiled=True)
    q_block = lax.dynamic_slice_in_dim(q_all, block_start, block_rows, 0).reshape(
        block_rows, heads_dev, HD
    )
    k_full = lax.all_gather(key_rows, "seq", axis=0, tiled=True)
    v_full = lax.all_gather(value_rows, "seq", axis=0, tiled=True)
    kv_head = seq_index * heads_dev // (head_total // kv_heads)
    k_all = lax.dynamic_slice_in_dim(k_full, kv_head * HD, HD, 1)
    v_all = lax.dynamic_slice_in_dim(v_full, kv_head * HD, HD, 1)
    key_pad = jnp.zeros((BAND, HD), BF)
    k_window = lax.dynamic_slice_in_dim(
        jnp.concatenate([key_pad, k_all], axis=0), block_start, BAND + block_rows, 0
    )
    v_window = lax.dynamic_slice_in_dim(
        jnp.concatenate([key_pad, v_all], axis=0), block_start, BAND + block_rows, 0
    )
    query_pos = block_start + jnp.arange(block_rows, dtype=jnp.int32)
    key_pos = block_start - BAND + jnp.arange(BAND + block_rows, dtype=jnp.int32)
    allowed = (
        (key_pos[None, :] <= query_pos[:, None])
        & (key_pos[None, :] > query_pos[:, None] - BAND)
        & (key_pos[None, :] >= 0)
    )
    scores = jnp.einsum("qhd,kd->hqk", q_block, k_window, preferred_element_type=F32) * HD ** (-0.5)
    scores = jnp.where(allowed[None, :, :], scores, -jnp.inf)
    attn_probs = jax.nn.softmax(scores, axis=-1).astype(BF)
    attn_out = jnp.einsum(
        "hqk,kd->qhd", attn_probs, v_window, preferred_element_type=F32
    ).astype(BF)
    return (moe_mixed, attn_out.reshape(block_rows, -1))


def pairs_of(lines, move):
    pairs = []
    for line in range(lines):
        for side in range(2):
            for lane in range(2):
                for core in range(2):
                    to = move(line, side, lane, core)
                    pairs.append(
                        (
                            (line * 2 + side) * 4 + lane * 2 + core,
                            (to[0] * 2 + to[1]) * 4 + to[2] * 2 + to[3],
                        )
                    )
    return pairs


def cols(array, start, size):
    return lax.dynamic_slice_in_dim(array, start, size, 1)


VMEM = pl.BlockSpec(memory_space=pltpu.VMEM)
HBM = pl.BlockSpec(memory_space=pltpu.HBM)
LIGHT = pl.CostEstimate(flops=0, bytes_accessed=1, transcendentals=0)
NT = (((1,), (1,)), ((), ()))
TABLE = 128
CHUNK = 384
AHEAD = 6


def block_of(number, size):
    return pl.ds(pl.multiple_of(number * size, size), size)


def place_here():
    place = lax.axis_index("expert")
    return place // 2, lax.rem(place, 2)


def rows_kernel(tokens, ids, weights, out):
    _, core = place_here()
    rows, width = out.shape[0], tokens.shape[1]
    out[:, :width] = tokens[block_of(core, rows), :]
    raw = weights[...]
    norm = (raw / jnp.sum(raw, axis=0, keepdims=True)).astype(BF).astype(F32)
    experts = 16 * ((EXP_SEQ * lax.axis_size("seq") + 15) // 16)
    number = lax.broadcasted_iota(jnp.int32, (experts, 2 * rows), 0)
    table = jnp.zeros((experts, 2 * rows), F32)
    for a in range(ids.shape[0]):
        table += jnp.where(number == ids[a : a + 1], norm[a : a + 1], 0.0)
    table = jnp.concatenate([table, jnp.zeros((TABLE - experts, 2 * rows), F32)], axis=0).T
    out[:, width:] = jnp.where(core == 0, table[:rows], table[rows:]).astype(BF)


def rows_of(tokens, ids, weights):
    rows, width = tokens.shape
    return pl.pallas_call(
        rows_kernel,
        cost_estimate=LIGHT,
        out_shape=jax.ShapeDtypeStruct((rows // 2, width + TABLE), BF),
        in_specs=[VMEM] * 3,
        out_specs=VMEM,
    )(tokens, ids.T, weights.T)


def expert_kernel(count, *refs):
    pieces, refs = refs[:count], refs[count:]
    gate_up, down = refs[:4], refs[4:6]
    opp_far_out, own_far_out, opp_out, own_out, rows_in, hidden = refs[6:]
    lane, _ = place_here()
    hid, width = gate_up[0].shape[1:]
    rows, size = pieces[0].shape[0], width // 2
    expert = EXP_SEQ * lax.axis_index("seq") + lane
    for number, piece in enumerate(pieces):
        rows_in[number * rows : (number + 1) * rows] = piece[:, :width]
    number = lax.broadcasted_iota(jnp.int32, (rows, TABLE), 1)
    scale = jnp.concatenate(
        [
            jnp.sum(
                jnp.where(number == expert, piece[:, width:].astype(F32), 0.0),
                axis=1,
                keepdims=True,
            )
            for piece in pieces
        ],
        axis=0,
    )
    for n in range(2):
        gate, up = (
            lax.dot_general(rows_in[...], gate_up[2 * n + i][0], NT, preferred_element_type=F32)
            for i in range(2)
        )
        hidden[:, n * hid : (n + 1) * hid] = (
            gate * (0.5 + 0.5 * jnp.tanh(0.5 * gate)) * up * scale
        ).astype(BF)
    many = count * rows // 2
    for column in (1 - lane, lane):
        value = 0.0
        for n in range(2):
            value += jnp.dot(
                hidden[:, n * hid : (n + 1) * hid],
                down[n][0, :, block_of(column, size)],
                preferred_element_type=F32,
            )
        if column is lane:
            own_out[...] = value[:many]
            opp_out[...] = value[many:]
        else:
            own_far_out[...] = value[:many].astype(BF)
            opp_far_out[...] = value[many:].astype(BF)


def expert_terms(pieces, *weights):
    count = len(pieces)
    rows = pieces[0].shape[0]
    hid, width = weights[0].shape[1:]
    shape = (count * rows // 2, width // 2)
    return pl.pallas_call(
        functools.partial(expert_kernel, count),
        cost_estimate=LIGHT,
        out_shape=tuple(jax.ShapeDtypeStruct(shape, kind) for kind in (BF, BF, F32, F32)),
        in_specs=[VMEM] * (count + 6),
        out_specs=(VMEM,) * 4,
        scratch_shapes=[
            pltpu.VMEM((count * rows, width), BF),
            pltpu.VMEM((count * rows, 2 * hid), BF),
        ],
        compiler_params=pltpu.CompilerParams(vmem_limit_bytes=32 << 20),
    )(*pieces, *weights)


def pack_kernel(keys, values, queries, gate, up, down, *refs):
    packets, pieces, sems = refs[:-3], refs[-3:-1], refs[-1]
    line, side = lax.axis_index("seq") // 2, lax.rem(lax.axis_index("seq"), 2)
    lane, core = place_here()
    size = pieces[0].shape[1]
    copies = []
    for m, piece in enumerate(pieces):
        block = 2 * (2 * core + lane) + lax.rem(side + m, 2)
        copies.append(
            pltpu.make_async_copy(queries.at[:, block_of(block, size)], piece, sems.at[m])
        )
    for copy in copies:
        copy.start()
    for k, packet in enumerate(packets):
        head = block_of(lax.rem(line + k, len(packets)), HD)
        packet[:, :HD] = keys[:, head]
        packet[:, HD:] = values[:, head]
    for copy in copies:
        copy.wait()


def packed(keys, values, queries, weights, lines):
    rows = keys.shape[0]
    packet = jax.ShapeDtypeStruct((rows, 2 * HD), BF)
    piece = jax.ShapeDtypeStruct((rows, queries.shape[1] // (2 * lines)), BF)
    return pl.pallas_call(
        pack_kernel,
        cost_estimate=LIGHT,
        out_shape=(packet,) * lines + (piece,) * 2,
        in_specs=[VMEM] * 2 + [HBM] + [VMEM] * 3,
        out_specs=(VMEM,) * (lines + 2),
        scratch_shapes=[pltpu.SemaphoreType.DMA((2,))],
        compiler_params=pltpu.CompilerParams(vmem_limit_bytes=24 << 20),
    )(keys, values, queries, *weights)


def attend_kernel(query_a, query_b, key_value, out, bias):
    rows = query_a.shape[0]
    blocks = key_value.shape[0] // rows
    line, side = lax.axis_index("seq") // 2, lax.rem(lax.axis_index("seq"), 2)
    keys, values = key_value[:, :HD], key_value[:, HD:]
    down = lax.broadcasted_iota(jnp.int32, (rows, rows), 0)
    along = lax.broadcasted_iota(jnp.int32, (rows, rows), 1)
    for number, query in enumerate((query_a, query_b)):
        upper = lax.rem(side + number, 2)
        at = 2 * lax.axis_index("expert") + upper
        for b in range(blocks):
            k, m = b // 2, b % 2
            behind = 2 * lax.rem(line + blocks // 2 - k, blocks // 2) + lax.rem(side + m, 2)
            behind = (at - behind) * rows + down - along
            bias[:, b * rows : (b + 1) * rows] = jnp.where(
                (behind >= 0) & (behind < BAND), 0.0, -1e30
            )
        target = block_of(upper, rows)
        for h in range(query.shape[1] // HD):
            head = slice(h * HD, (h + 1) * HD)
            scores = lax.dot_general(
                query[:, head], keys, (((1,), (1,)), ((), ())), preferred_element_type=F32
            )
            scores = scores * HD ** (-0.5) + bias[...]
            probs = jnp.exp(scores - jnp.max(scores, axis=1, keepdims=True))
            total = jnp.sum(probs, axis=1, keepdims=True)
            mixed = jnp.dot(probs.astype(BF), values, preferred_element_type=F32)
            out[target, head] = (mixed / total).astype(BF)


def attended(query_a, query_b, key_value):
    rows, width = query_a.shape
    count = key_value.shape[0]
    return pl.pallas_call(
        attend_kernel,
        cost_estimate=LIGHT,
        out_shape=jax.ShapeDtypeStruct((2 * rows, width), BF),
        in_specs=[VMEM] * 3,
        out_specs=VMEM,
        scratch_shapes=[pltpu.VMEM((rows, count), F32)],
        compiler_params=pltpu.CompilerParams(vmem_limit_bytes=24 << 20),
    )(query_a, query_b, key_value)


def lane_body(
    tokens, expert_ids, route_weights, w_gate, w_up, w_down, query_rows, key_rows, value_rows
):
    seq_index = lax.axis_index("seq")
    expert_index = lax.axis_index("expert")
    lines = lax.axis_size("seq") // 2
    side = seq_index % 2
    lane, core = expert_index // 2, expert_index % 2
    rows, width = tokens.shape
    quarter = width // 4

    routes = {
        "core": pairs_of(lines, lambda l, s, n, c: (l, s, n, 1 - c)),
        "lane": pairs_of(lines, lambda l, s, n, c: (l, s, 1 - n, c)),
    }
    for k in range(lines):
        for m in range(2):
            routes[k, m] = pairs_of(
                lines, lambda l, s, n, c: ((l + k) % lines, (s + m) % 2, n, c)
            )
            routes["query", m] = pairs_of(
                lines, lambda l, s, n, c: (2 * c + n, (s + m) % 2, l // 2, l % 2)
            )
    flight = {}
    now = [jnp.zeros((), F32)]

    def at(value):
        value, now[0] = lax.optimization_barrier((value, now[0]))
        return value

    def start(name, value, route):
        with jax.named_scope("send_" + name):
            flight[name] = lax.ppermute(at(value), AXES, routes[route])

    def done(name):
        return at(flight.pop(name))

    own, opp, parts, moe = {}, {}, {}, {}
    half = rows // 2

    def expert_on(k):
        parts[k] = at(expert_terms([own[k], opp[k]], w_gate, w_up, wg, wu, w_down, wd))

    def to_side(k):
        summed = parts[k][2] + done(f"rx{k}").astype(F32)
        start(f"ry{k}", summed.astype(BF), (0, 1))

    def lane_start(k):
        start(f"rw{k}", parts[k][1], "lane")

    def lane_done(k):
        moe[k] = moe.get(k, parts[k][3]) + done(f"rw{k}").astype(F32)

    def side_done(k):
        moe[k] = moe.get(k, parts[k][3]) + done(f"ry{k}").astype(F32)

    own[0] = at(rows_of(tokens, expert_ids, route_weights))
    start("z1", own[0], (1, 0))
    start("y0", own[0], (0, 1))
    start("wg", w_gate, "core")
    start("wu", w_up, "core")
    *packets, query_a, query_b = at(
        packed(key_rows, value_rows, query_rows, (w_gate, w_up, w_down), lines)
    )
    start("kz1", packets[1], (1, 0))
    packets[1] = done("kz1")
    own[1] = done("z1")
    opp[0] = done("y0")
    wg = done("wg")
    wu = done("wu")
    start("z2", own[1], (1, 0))
    start("y1", own[1], (0, 1))
    start("wd", w_down, "core")
    start("q0", query_a, ("query", 0))
    wd = done("wd")
    expert_on(0)
    opp[1] = done("y1")
    own[2] = done("z2")
    query_a = done("q0")
    start("y2", own[2], (0, 1))
    start("z3", own[0], (3, 0))
    start("rx0", parts[0][0], "lane")
    for k in (2, 3):
        start(f"kz{k}", packets[k], (k, 0))
    expert_on(1)
    opp[2] = done("y2")
    own[3] = done("z3")
    for k in (2, 3):
        packets[k] = done(f"kz{k}")
    small = at(jnp.stack(packets))
    to_side(0)
    start("y3", own[3], (0, 1))
    start("rx1", parts[1][0], "lane")
    lane_start(1)
    start("q1", query_b, ("query", 1))
    expert_on(2)
    opp[3] = done("y3")
    start("rx2", parts[2][0], "lane")
    expert_on(3)
    side_done(0)
    lane_done(1)
    start("rx3", parts[3][0], "lane")
    to_side(1)
    to_side(2)
    lane_start(2)
    query_b = done("q1")
    start("ky", small, (0, 1))
    to_side(3)
    lane_start(3)
    side_done(1)
    start("rz1", moe[1].astype(BF), (3, 0))
    side_done(2)
    lane_done(2)
    start("rz2", moe[2].astype(BF), (1, 0))
    key_value = jnp.stack([small, done("ky")], axis=1).reshape(2 * lines * rows, 2 * HD)
    side_done(3)
    lane_done(3)
    lane_start(0)
    block = (moe[3] + done("rz2").astype(F32)).astype(BF)
    start("rz3", block, (1, 0))
    attn_out = at(attended(query_a, query_b, key_value))
    lane_done(0)
    total = moe[0] + done("rz1").astype(F32)
    total = (total + done("rz3").astype(F32)).astype(BF)
    kept, passed = (cols(total, c * quarter, quarter) for c in (core, 1 - core))
    start("last", passed, "core")
    passed = done("last")
    moe_mixed = jnp.concatenate(
        [jnp.where(core == 0, kept, passed), jnp.where(core == 0, passed, kept)], axis=0
    )
    return (moe_mixed + now[0].astype(BF), attn_out)


def solution(mesh):
    placed = (
        P("seq", None),
        P("seq", None),
        P("seq", None),
        P(("seq", "expert"), None, None),
        P(("seq", "expert"), None, None),
        P(("seq", "expert"), None, None),
        P("seq", None),
        P("seq", None),
        P("seq", None),
    )
    fits = mesh.shape["expert"] == 4 and mesh.shape["seq"] == 8
    return jax.shard_map(
        lane_body if fits else general_body,
        mesh=mesh,
        in_specs=placed,
        out_specs=(P("seq", "expert"), P("expert", "seq")),
        check_vma=False,
    )
```

```python
import functools

import jax
import jax.numpy as jnp
from jax import lax
from jax.experimental import pallas as pl
from jax.experimental.pallas import tpu as pltpu
from jax.sharding import PartitionSpec as P

HD = 128
BAND = 1024
EXP_SEQ = 2
AXES = ("seq", "expert")
BF = jnp.bfloat16
F32 = jnp.float32
LIMIT = 56 << 20


def general_body(
    tokens, expert_ids, route_weights, w_gate, w_up, w_down, query_rows, key_rows, value_rows
):
    seq_index = lax.axis_index("seq")
    expert_index = lax.axis_index("expert")
    seq_count = lax.axis_size("seq")
    expert_count = lax.axis_size("expert")
    slice_count = expert_count // EXP_SEQ
    half_index = expert_index // slice_count
    tok_rows, width = tokens.shape
    route_count = expert_ids.shape[1]
    capacity = 3 * tok_rows * route_count // (2 * EXP_SEQ * seq_count)
    norm_weights = (route_weights / jnp.sum(route_weights, axis=1, keepdims=True)).astype(BF)
    targets = jnp.arange(seq_count, dtype=jnp.int32) * EXP_SEQ + half_index
    matched = expert_ids[:, :, None] == targets[None, None, :]
    routed_hit = jnp.sum(matched.astype(F32), axis=1)
    picked = jnp.sum(
        jnp.where(matched, norm_weights.astype(F32)[:, :, None], jnp.float32(0.0)), axis=1
    )
    row_ids = jnp.arange(tok_rows, dtype=jnp.int32)
    earlier = (row_ids[:, None] > row_ids[None, :]).astype(F32)
    slot_rank = jnp.dot(earlier, routed_hit, precision=lax.Precision.HIGHEST)
    slot_ids = jnp.arange(capacity, dtype=F32)
    onehot = (slot_rank.T[:, None, :] == slot_ids[None, :, None]) & (
        routed_hit.T[:, None, :] > 0.5
    )
    selector = onehot.astype(BF)
    outgoing = jnp.einsum("jct,td->jcd", selector, tokens, preferred_element_type=F32).astype(BF)
    incoming = lax.all_to_all(outgoing, "seq", split_axis=0, concat_axis=0, tiled=True)
    slot_count = incoming.shape[1]
    flat_rows = incoming.reshape(-1, width)
    nt = (((1,), (1,)), ((), ()))
    gate_out = lax.dot_general(flat_rows, w_gate[0], nt, preferred_element_type=F32)
    up_out = lax.dot_general(flat_rows, w_up[0], nt, preferred_element_type=F32)
    hidden = (jax.nn.silu(gate_out) * up_out).astype(BF)
    partial_value = jnp.dot(hidden, w_down[0], preferred_element_type=F32).astype(BF)
    partial_value = partial_value.reshape(seq_count, slot_count, width)
    returned = lax.all_to_all(partial_value, "seq", split_axis=0, concat_axis=0, tiled=True)
    combine = (onehot.astype(F32) * picked.T[:, None, :]).astype(BF)
    local_term = jnp.einsum("jct,jcd->td", combine, returned, preferred_element_type=F32)
    moe_mixed = lax.psum_scatter(local_term, "expert", scatter_dimension=1, tiled=True).astype(BF)
    head_total = query_rows.shape[1] // HD
    kv_heads = key_rows.shape[1] // HD
    heads_dev = head_total // seq_count
    block_rows = tok_rows * seq_count // expert_count
    block_start = expert_index * block_rows
    q_all = lax.all_to_all(query_rows, "seq", split_axis=1, concat_axis=0, tiled=True)
    q_block = lax.dynamic_slice_in_dim(q_all, block_start, block_rows, 0).reshape(
        block_rows, heads_dev, HD
    )
    k_full = lax.all_gather(key_rows, "seq", axis=0, tiled=True)
    v_full = lax.all_gather(value_rows, "seq", axis=0, tiled=True)
    kv_head = seq_index * heads_dev // (head_total // kv_heads)
    k_all = lax.dynamic_slice_in_dim(k_full, kv_head * HD, HD, 1)
    v_all = lax.dynamic_slice_in_dim(v_full, kv_head * HD, HD, 1)
    key_pad = jnp.zeros((BAND, HD), BF)
    k_window = lax.dynamic_slice_in_dim(
        jnp.concatenate([key_pad, k_all], axis=0), block_start, BAND + block_rows, 0
    )
    v_window = lax.dynamic_slice_in_dim(
        jnp.concatenate([key_pad, v_all], axis=0), block_start, BAND + block_rows, 0
    )
    query_pos = block_start + jnp.arange(block_rows, dtype=jnp.int32)
    key_pos = block_start - BAND + jnp.arange(BAND + block_rows, dtype=jnp.int32)
    allowed = (
        (key_pos[None, :] <= query_pos[:, None])
        & (key_pos[None, :] > query_pos[:, None] - BAND)
        & (key_pos[None, :] >= 0)
    )
    scores = jnp.einsum("qhd,kd->hqk", q_block, k_window, preferred_element_type=F32) * HD ** (-0.5)
    scores = jnp.where(allowed[None, :, :], scores, -jnp.inf)
    attn_probs = jax.nn.softmax(scores, axis=-1).astype(BF)
    attn_out = jnp.einsum(
        "hqk,kd->qhd", attn_probs, v_window, preferred_element_type=F32
    ).astype(BF)
    return (moe_mixed, attn_out.reshape(block_rows, -1))


def pairs_of(lines, move):
    pairs = []
    for line in range(lines):
        for side in range(2):
            for lane in range(2):
                for core in range(2):
                    to = move(line, side, lane, core)
                    pairs.append(
                        (
                            (line * 2 + side) * 4 + lane * 2 + core,
                            (to[0] * 2 + to[1]) * 4 + to[2] * 2 + to[3],
                        )
                    )
    return pairs


def cols(array, start, size):
    return lax.dynamic_slice_in_dim(array, start, size, 1)


VMEM = pl.BlockSpec(memory_space=pltpu.VMEM)
HBM = pl.BlockSpec(memory_space=pltpu.HBM)
LIGHT = pl.CostEstimate(flops=0, bytes_accessed=1, transcendentals=0)
NT = (((1,), (1,)), ((), ()))
TABLE = 128
CHUNK = 384
AHEAD = 6


def block_of(number, size):
    return pl.ds(pl.multiple_of(number * size, size), size)


def place_here():
    place = lax.axis_index("expert")
    return place // 2, lax.rem(place, 2)


def rows_kernel(tokens, ids, weights, out):
    _, core = place_here()
    rows, width = out.shape[0], tokens.shape[1]
    out[:, :width] = tokens[block_of(core, rows), :]
    raw = weights[...]
    norm = (raw / jnp.sum(raw, axis=0, keepdims=True)).astype(BF).astype(F32)
    experts = 16 * ((EXP_SEQ * lax.axis_size("seq") + 15) // 16)
    number = lax.broadcasted_iota(jnp.int32, (experts, 2 * rows), 0)
    table = jnp.zeros((experts, 2 * rows), F32)
    for a in range(ids.shape[0]):
        table += jnp.where(number == ids[a : a + 1], norm[a : a + 1], 0.0)
    table = jnp.concatenate([table, jnp.zeros((TABLE - experts, 2 * rows), F32)], axis=0).T
    out[:, width:] = jnp.where(core == 0, table[:rows], table[rows:]).astype(BF)


def rows_of(tokens, ids, weights):
    rows, width = tokens.shape
    return pl.pallas_call(
        rows_kernel,
        cost_estimate=LIGHT,
        out_shape=jax.ShapeDtypeStruct((rows // 2, width + TABLE), BF),
        in_specs=[VMEM] * 3,
        out_specs=VMEM,
    )(tokens, ids.T, weights.T)


def expert_kernel(count, *refs):
    pieces, refs = refs[:count], refs[count:]
    gate_up, down = refs[:4], refs[4:6]
    opp_far_out, own_far_out, opp_out, own_out, rows_in, hidden = refs[6:]
    lane, _ = place_here()
    hid, width = gate_up[0].shape[1:]
    rows, size = pieces[0].shape[0], width // 2
    expert = EXP_SEQ * lax.axis_index("seq") + lane
    for number, piece in enumerate(pieces):
        rows_in[number * rows : (number + 1) * rows] = piece[:, :width]
    number = lax.broadcasted_iota(jnp.int32, (rows, TABLE), 1)
    scale = jnp.concatenate(
        [
            jnp.sum(
                jnp.where(number == expert, piece[:, width:].astype(F32), 0.0),
                axis=1,
                keepdims=True,
            )
            for piece in pieces
        ],
        axis=0,
    )
    for n in range(2):
        gate, up = (
            lax.dot_general(rows_in[...], gate_up[2 * n + i][0], NT, preferred_element_type=F32)
            for i in range(2)
        )
        hidden[:, n * hid : (n + 1) * hid] = (
            gate * (0.5 + 0.5 * jnp.tanh(0.5 * gate)) * up * scale
        ).astype(BF)
    many = count * rows // 2
    for column in (1 - lane, lane):
        value = 0.0
        for n in range(2):
            value += jnp.dot(
                hidden[:, n * hid : (n + 1) * hid],
                down[n][0, :, block_of(column, size)],
                preferred_element_type=F32,
            )
        if column is lane:
            own_out[...] = value[:many]
            opp_out[...] = value[many:]
        else:
            own_far_out[...] = value[:many].astype(BF)
            opp_far_out[...] = value[many:].astype(BF)


def expert_terms(pieces, *weights):
    count = len(pieces)
    rows = pieces[0].shape[0]
    hid, width = weights[0].shape[1:]
    shape = (count * rows // 2, width // 2)
    return pl.pallas_call(
        functools.partial(expert_kernel, count),
        cost_estimate=LIGHT,
        out_shape=tuple(jax.ShapeDtypeStruct(shape, kind) for kind in (BF, BF, F32, F32)),
        in_specs=[VMEM] * (count + 6),
        out_specs=(VMEM,) * 4,
        scratch_shapes=[
            pltpu.VMEM((count * rows, width), BF),
            pltpu.VMEM((count * rows, 2 * hid), BF),
        ],
        compiler_params=pltpu.CompilerParams(vmem_limit_bytes=32 << 20),
    )(*pieces, *weights)


def pack_kernel(keys, values, queries, gate, up, down, *refs):
    packets, pieces, sems = refs[:-3], refs[-3:-1], refs[-1]
    line, side = lax.axis_index("seq") // 2, lax.rem(lax.axis_index("seq"), 2)
    lane, core = place_here()
    size = pieces[0].shape[1]
    copies = []
    for m, piece in enumerate(pieces):
        block = 2 * (2 * core + lane) + lax.rem(side + m, 2)
        copies.append(
            pltpu.make_async_copy(queries.at[:, block_of(block, size)], piece, sems.at[m])
        )
    for copy in copies:
        copy.start()
    for k, packet in enumerate(packets):
        head = block_of(lax.rem(line + k, len(packets)), HD)
        packet[:, :HD] = keys[:, head]
        packet[:, HD:] = values[:, head]
    for copy in copies:
        copy.wait()


def packed(keys, values, queries, weights, lines):
    rows = keys.shape[0]
    packet = jax.ShapeDtypeStruct((rows, 2 * HD), BF)
    piece = jax.ShapeDtypeStruct((rows, queries.shape[1] // (2 * lines)), BF)
    return pl.pallas_call(
        pack_kernel,
        cost_estimate=LIGHT,
        out_shape=(packet,) * lines + (piece,) * 2,
        in_specs=[VMEM] * 2 + [HBM] + [VMEM] * 3,
        out_specs=(VMEM,) * (lines + 2),
        scratch_shapes=[pltpu.SemaphoreType.DMA((2,))],
        compiler_params=pltpu.CompilerParams(vmem_limit_bytes=24 << 20),
    )(keys, values, queries, *weights)


def attend_kernel(query_a, query_b, key_value, out, bias):
    rows = query_a.shape[0]
    blocks = key_value.shape[0] // rows
    line, side = lax.axis_index("seq") // 2, lax.rem(lax.axis_index("seq"), 2)
    keys, values = key_value[:, :HD], key_value[:, HD:]
    down = lax.broadcasted_iota(jnp.int32, (rows, rows), 0)
    along = lax.broadcasted_iota(jnp.int32, (rows, rows), 1)
    for number, query in enumerate((query_a, query_b)):
        upper = lax.rem(side + number, 2)
        at = 2 * lax.axis_index("expert") + upper
        for b in range(blocks):
            k, m = b // 2, b % 2
            behind = 2 * lax.rem(line + blocks // 2 - k, blocks // 2) + lax.rem(side + m, 2)
            behind = (at - behind) * rows + down - along
            bias[:, b * rows : (b + 1) * rows] = jnp.where(
                (behind >= 0) & (behind < BAND), 0.0, -1e30
            )
        target = block_of(upper, rows)
        for h in range(query.shape[1] // HD):
            head = slice(h * HD, (h + 1) * HD)
            scores = lax.dot_general(
                query[:, head], keys, (((1,), (1,)), ((), ())), preferred_element_type=F32
            )
            scores = scores * HD ** (-0.5) + bias[...]
            probs = jnp.exp(scores - jnp.max(scores, axis=1, keepdims=True))
            total = jnp.sum(probs, axis=1, keepdims=True)
            mixed = jnp.dot(probs.astype(BF), values, preferred_element_type=F32)
            out[target, head] = (mixed / total).astype(BF)


def attended(query_a, query_b, key_value):
    rows, width = query_a.shape
    count = key_value.shape[0]
    return pl.pallas_call(
        attend_kernel,
        cost_estimate=LIGHT,
        out_shape=jax.ShapeDtypeStruct((2 * rows, width), BF),
        in_specs=[VMEM] * 3,
        out_specs=VMEM,
        scratch_shapes=[pltpu.VMEM((rows, count), F32)],
        compiler_params=pltpu.CompilerParams(vmem_limit_bytes=24 << 20),
    )(query_a, query_b, key_value)


def lane_body(
    tokens, expert_ids, route_weights, w_gate, w_up, w_down, query_rows, key_rows, value_rows
):
    seq_index = lax.axis_index("seq")
    expert_index = lax.axis_index("expert")
    lines = lax.axis_size("seq") // 2
    side = seq_index % 2
    lane, core = expert_index // 2, expert_index % 2
    rows, width = tokens.shape
    quarter = width // 4

    routes = {
        "core": pairs_of(lines, lambda l, s, n, c: (l, s, n, 1 - c)),
        "lane": pairs_of(lines, lambda l, s, n, c: (l, s, 1 - n, c)),
    }
    for k in range(lines):
        for m in range(2):
            routes[k, m] = pairs_of(
                lines, lambda l, s, n, c: ((l + k) % lines, (s + m) % 2, n, c)
            )
            routes["query", m] = pairs_of(
                lines, lambda l, s, n, c: (2 * c + n, (s + m) % 2, l // 2, l % 2)
            )
    flight = {}
    now = [jnp.zeros((), F32)]

    def at(value):
        value, now[0] = lax.optimization_barrier((value, now[0]))
        return value

    def start(name, value, route):
        with jax.named_scope("send_" + name):
            flight[name] = lax.ppermute(at(value), AXES, routes[route])

    def done(name):
        return at(flight.pop(name))

    own, opp, parts, moe = {}, {}, {}, {}
    half = rows // 2

    def expert_on(k):
        parts[k] = at(expert_terms([own[k], opp[k]], w_gate, w_up, wg, wu, w_down, wd))

    def to_side(k):
        summed = parts[k][2] + done(f"rx{k}").astype(F32)
        start(f"ry{k}", summed.astype(BF), (0, 1))

    def lane_start(k):
        start(f"rw{k}", parts[k][1], "lane")

    def lane_done(k):
        moe[k] = moe.get(k, parts[k][3]) + done(f"rw{k}").astype(F32)

    def side_done(k):
        moe[k] = moe.get(k, parts[k][3]) + done(f"ry{k}").astype(F32)

    own[0] = at(rows_of(tokens, expert_ids, route_weights))
    start("z1", own[0], (1, 0))
    start("y0", own[0], (0, 1))
    start("wg", w_gate, "core")
    start("wu", w_up, "core")
    *packets, query_a, query_b = at(
        packed(key_rows, value_rows, query_rows, (w_gate, w_up, w_down), lines)
    )
    start("kz1", packets[1], (1, 0))
    packets[1] = done("kz1")
    own[1] = done("z1")
    opp[0] = done("y0")
    wg = done("wg")
    wu = done("wu")
    start("z2", own[1], (1, 0))
    start("y1", own[1], (0, 1))
    start("wd", w_down, "core")
    start("q0", query_a, ("query", 0))
    wd = done("wd")
    expert_on(0)
    opp[1] = done("y1")
    own[2] = done("z2")
    query_a = done("q0")
    start("y2", own[2], (0, 1))
    start("z3", own[0], (3, 0))
    start("rx0", parts[0][0], "lane")
    for k in (2, 3):
        start(f"kz{k}", packets[k], (k, 0))
    expert_on(1)
    own[3] = done("z3")
    opp[2] = done("y2")
    for k in (2, 3):
        packets[k] = done(f"kz{k}")
    small = at(jnp.stack(packets))
    to_side(0)
    start("y3", own[3], (0, 1))
    start("rx1", parts[1][0], "lane")
    lane_start(1)
    start("q1", query_b, ("query", 1))
    expert_on(2)
    opp[3] = done("y3")
    start("rx2", parts[2][0], "lane")
    expert_on(3)
    side_done(0)
    lane_done(1)
    start("rx3", parts[3][0], "lane")
    to_side(1)
    to_side(2)
    lane_start(2)
    query_b = done("q1")
    start("ky", small, (0, 1))
    to_side(3)
    lane_start(3)
    side_done(1)
    start("rz1", moe[1].astype(BF), (3, 0))
    side_done(2)
    lane_done(2)
    start("rz2", moe[2].astype(BF), (1, 0))
    key_value = jnp.stack([small, done("ky")], axis=1).reshape(2 * lines * rows, 2 * HD)
    side_done(3)
    lane_done(3)
    lane_start(0)
    block = (moe[3] + done("rz2").astype(F32)).astype(BF)
    start("rz3", block, (1, 0))
    attn_out = at(attended(query_a, query_b, key_value))
    lane_done(0)
    total = moe[0] + done("rz1").astype(F32)
    total = (total + done("rz3").astype(F32)).astype(BF)
    kept, passed = (cols(total, c * quarter, quarter) for c in (core, 1 - core))
    start("last", passed, "core")
    passed = done("last")
    moe_mixed = jnp.concatenate(
        [jnp.where(core == 0, kept, passed), jnp.where(core == 0, passed, kept)], axis=0
    )
    return (moe_mixed + now[0].astype(BF), attn_out)


def solution(mesh):
    placed = (
        P("seq", None),
        P("seq", None),
        P("seq", None),
        P(("seq", "expert"), None, None),
        P(("seq", "expert"), None, None),
        P(("seq", "expert"), None, None),
        P("seq", None),
        P("seq", None),
        P("seq", None),
    )
    fits = mesh.shape["expert"] == 4 and mesh.shape["seq"] == 8
    return jax.shard_map(
        lane_body if fits else general_body,
        mesh=mesh,
        in_specs=placed,
        out_specs=(P("seq", "expert"), P("expert", "seq")),
        check_vma=False,
    )
```

```python
import functools

import jax
import jax.numpy as jnp
from jax import lax
from jax.experimental import pallas as pl
from jax.experimental.pallas import tpu as pltpu
from jax.sharding import PartitionSpec as P

HD = 128
BAND = 1024
EXP_SEQ = 2
AXES = ("seq", "expert")
BF = jnp.bfloat16
F32 = jnp.float32
LIMIT = 56 << 20


def general_body(
    tokens, expert_ids, route_weights, w_gate, w_up, w_down, query_rows, key_rows, value_rows
):
    seq_index = lax.axis_index("seq")
    expert_index = lax.axis_index("expert")
    seq_count = lax.axis_size("seq")
    expert_count = lax.axis_size("expert")
    slice_count = expert_count // EXP_SEQ
    half_index = expert_index // slice_count
    tok_rows, width = tokens.shape
    route_count = expert_ids.shape[1]
    capacity = 3 * tok_rows * route_count // (2 * EXP_SEQ * seq_count)
    norm_weights = (route_weights / jnp.sum(route_weights, axis=1, keepdims=True)).astype(BF)
    targets = jnp.arange(seq_count, dtype=jnp.int32) * EXP_SEQ + half_index
    matched = expert_ids[:, :, None] == targets[None, None, :]
    routed_hit = jnp.sum(matched.astype(F32), axis=1)
    picked = jnp.sum(
        jnp.where(matched, norm_weights.astype(F32)[:, :, None], jnp.float32(0.0)), axis=1
    )
    row_ids = jnp.arange(tok_rows, dtype=jnp.int32)
    earlier = (row_ids[:, None] > row_ids[None, :]).astype(F32)
    slot_rank = jnp.dot(earlier, routed_hit, precision=lax.Precision.HIGHEST)
    slot_ids = jnp.arange(capacity, dtype=F32)
    onehot = (slot_rank.T[:, None, :] == slot_ids[None, :, None]) & (
        routed_hit.T[:, None, :] > 0.5
    )
    selector = onehot.astype(BF)
    outgoing = jnp.einsum("jct,td->jcd", selector, tokens, preferred_element_type=F32).astype(BF)
    incoming = lax.all_to_all(outgoing, "seq", split_axis=0, concat_axis=0, tiled=True)
    slot_count = incoming.shape[1]
    flat_rows = incoming.reshape(-1, width)
    nt = (((1,), (1,)), ((), ()))
    gate_out = lax.dot_general(flat_rows, w_gate[0], nt, preferred_element_type=F32)
    up_out = lax.dot_general(flat_rows, w_up[0], nt, preferred_element_type=F32)
    hidden = (jax.nn.silu(gate_out) * up_out).astype(BF)
    partial_value = jnp.dot(hidden, w_down[0], preferred_element_type=F32).astype(BF)
    partial_value = partial_value.reshape(seq_count, slot_count, width)
    returned = lax.all_to_all(partial_value, "seq", split_axis=0, concat_axis=0, tiled=True)
    combine = (onehot.astype(F32) * picked.T[:, None, :]).astype(BF)
    local_term = jnp.einsum("jct,jcd->td", combine, returned, preferred_element_type=F32)
    moe_mixed = lax.psum_scatter(local_term, "expert", scatter_dimension=1, tiled=True).astype(BF)
    head_total = query_rows.shape[1] // HD
    kv_heads = key_rows.shape[1] // HD
    heads_dev = head_total // seq_count
    block_rows = tok_rows * seq_count // expert_count
    block_start = expert_index * block_rows
    q_all = lax.all_to_all(query_rows, "seq", split_axis=1, concat_axis=0, tiled=True)
    q_block = lax.dynamic_slice_in_dim(q_all, block_start, block_rows, 0).reshape(
        block_rows, heads_dev, HD
    )
    k_full = lax.all_gather(key_rows, "seq", axis=0, tiled=True)
    v_full = lax.all_gather(value_rows, "seq", axis=0, tiled=True)
    kv_head = seq_index * heads_dev // (head_total // kv_heads)
    k_all = lax.dynamic_slice_in_dim(k_full, kv_head * HD, HD, 1)
    v_all = lax.dynamic_slice_in_dim(v_full, kv_head * HD, HD, 1)
    key_pad = jnp.zeros((BAND, HD), BF)
    k_window = lax.dynamic_slice_in_dim(
        jnp.concatenate([key_pad, k_all], axis=0), block_start, BAND + block_rows, 0
    )
    v_window = lax.dynamic_slice_in_dim(
        jnp.concatenate([key_pad, v_all], axis=0), block_start, BAND + block_rows, 0
    )
    query_pos = block_start + jnp.arange(block_rows, dtype=jnp.int32)
    key_pos = block_start - BAND + jnp.arange(BAND + block_rows, dtype=jnp.int32)
    allowed = (
        (key_pos[None, :] <= query_pos[:, None])
        & (key_pos[None, :] > query_pos[:, None] - BAND)
        & (key_pos[None, :] >= 0)
    )
    scores = jnp.einsum("qhd,kd->hqk", q_block, k_window, preferred_element_type=F32) * HD ** (-0.5)
    scores = jnp.where(allowed[None, :, :], scores, -jnp.inf)
    attn_probs = jax.nn.softmax(scores, axis=-1).astype(BF)
    attn_out = jnp.einsum(
        "hqk,kd->qhd", attn_probs, v_window, preferred_element_type=F32
    ).astype(BF)
    return (moe_mixed, attn_out.reshape(block_rows, -1))


def pairs_of(lines, move):
    pairs = []
    for line in range(lines):
        for side in range(2):
            for lane in range(2):
                for core in range(2):
                    to = move(line, side, lane, core)
                    pairs.append(
                        (
                            (line * 2 + side) * 4 + lane * 2 + core,
                            (to[0] * 2 + to[1]) * 4 + to[2] * 2 + to[3],
                        )
                    )
    return pairs


def cols(array, start, size):
    return lax.dynamic_slice_in_dim(array, start, size, 1)


VMEM = pl.BlockSpec(memory_space=pltpu.VMEM)
HBM = pl.BlockSpec(memory_space=pltpu.HBM)
LIGHT = pl.CostEstimate(flops=0, bytes_accessed=1, transcendentals=0)
NT = (((1,), (1,)), ((), ()))
TABLE = 128
CHUNK = 384
AHEAD = 6


def block_of(number, size):
    return pl.ds(pl.multiple_of(number * size, size), size)


def place_here():
    place = lax.axis_index("expert")
    return place // 2, lax.rem(place, 2)


def rows_kernel(tokens, ids, weights, out):
    _, core = place_here()
    rows, width = out.shape[0], tokens.shape[1]
    out[:, :width] = tokens[block_of(core, rows), :]
    raw = weights[...]
    norm = (raw / jnp.sum(raw, axis=0, keepdims=True)).astype(BF).astype(F32)
    experts = 16 * ((EXP_SEQ * lax.axis_size("seq") + 15) // 16)
    number = lax.broadcasted_iota(jnp.int32, (experts, 2 * rows), 0)
    table = jnp.zeros((experts, 2 * rows), F32)
    for a in range(ids.shape[0]):
        table += jnp.where(number == ids[a : a + 1], norm[a : a + 1], 0.0)
    table = jnp.concatenate([table, jnp.zeros((TABLE - experts, 2 * rows), F32)], axis=0).T
    out[:, width:] = jnp.where(core == 0, table[:rows], table[rows:]).astype(BF)


def rows_of(tokens, ids, weights):
    rows, width = tokens.shape
    return pl.pallas_call(
        rows_kernel,
        cost_estimate=LIGHT,
        out_shape=jax.ShapeDtypeStruct((rows // 2, width + TABLE), BF),
        in_specs=[VMEM] * 3,
        out_specs=VMEM,
    )(tokens, ids.T, weights.T)


def expert_kernel(count, *refs):
    pieces, refs = refs[:count], refs[count:]
    gate_up, down = refs[:4], refs[4:6]
    opp_far_out, own_far_out, opp_out, own_out, rows_in, hidden = refs[6:]
    lane, _ = place_here()
    hid, width = gate_up[0].shape[1:]
    rows, size = pieces[0].shape[0], width // 2
    expert = EXP_SEQ * lax.axis_index("seq") + lane
    for number, piece in enumerate(pieces):
        rows_in[number * rows : (number + 1) * rows] = piece[:, :width]
    number = lax.broadcasted_iota(jnp.int32, (rows, TABLE), 1)
    scale = jnp.concatenate(
        [
            jnp.sum(
                jnp.where(number == expert, piece[:, width:].astype(F32), 0.0),
                axis=1,
                keepdims=True,
            )
            for piece in pieces
        ],
        axis=0,
    )
    for n in range(2):
        gate, up = (
            lax.dot_general(rows_in[...], gate_up[2 * n + i][0], NT, preferred_element_type=F32)
            for i in range(2)
        )
        hidden[:, n * hid : (n + 1) * hid] = (
            gate * (0.5 + 0.5 * jnp.tanh(0.5 * gate)) * up * scale
        ).astype(BF)
    many = count * rows // 2
    for column in (1 - lane, lane):
        value = 0.0
        for n in range(2):
            value += jnp.dot(
                hidden[:, n * hid : (n + 1) * hid],
                down[n][0, :, block_of(column, size)],
                preferred_element_type=F32,
            )
        if column is lane:
            own_out[...] = value[:many]
            opp_out[...] = value[many:]
        else:
            own_far_out[...] = value[:many].astype(BF)
            opp_far_out[...] = value[many:].astype(BF)


def expert_terms(pieces, *weights):
    count = len(pieces)
    rows = pieces[0].shape[0]
    hid, width = weights[0].shape[1:]
    shape = (count * rows // 2, width // 2)
    return pl.pallas_call(
        functools.partial(expert_kernel, count),
        cost_estimate=LIGHT,
        out_shape=tuple(jax.ShapeDtypeStruct(shape, kind) for kind in (BF, BF, F32, F32)),
        in_specs=[VMEM] * (count + 6),
        out_specs=(VMEM,) * 4,
        scratch_shapes=[
            pltpu.VMEM((count * rows, width), BF),
            pltpu.VMEM((count * rows, 2 * hid), BF),
        ],
        compiler_params=pltpu.CompilerParams(vmem_limit_bytes=32 << 20),
    )(*pieces, *weights)


def pack_kernel(keys, values, queries, gate, up, down, *refs):
    packets, pieces, sems = refs[:-3], refs[-3:-1], refs[-1]
    line, side = lax.axis_index("seq") // 2, lax.rem(lax.axis_index("seq"), 2)
    lane, core = place_here()
    size = pieces[0].shape[1]
    copies = []
    for m, piece in enumerate(pieces):
        block = 2 * (2 * core + lane) + lax.rem(side + m, 2)
        copies.append(
            pltpu.make_async_copy(queries.at[:, block_of(block, size)], piece, sems.at[m])
        )
    for copy in copies:
        copy.start()
    for k, packet in enumerate(packets):
        head = block_of(lax.rem(line + k, len(packets)), HD)
        packet[:, :HD] = keys[:, head]
        packet[:, HD:] = values[:, head]
    for copy in copies:
        copy.wait()


def packed(keys, values, queries, weights, lines):
    rows = keys.shape[0]
    packet = jax.ShapeDtypeStruct((rows, 2 * HD), BF)
    piece = jax.ShapeDtypeStruct((rows, queries.shape[1] // (2 * lines)), BF)
    return pl.pallas_call(
        pack_kernel,
        cost_estimate=LIGHT,
        out_shape=(packet,) * lines + (piece,) * 2,
        in_specs=[VMEM] * 2 + [HBM] + [VMEM] * 3,
        out_specs=(VMEM,) * (lines + 2),
        scratch_shapes=[pltpu.SemaphoreType.DMA((2,))],
        compiler_params=pltpu.CompilerParams(vmem_limit_bytes=24 << 20),
    )(keys, values, queries, *weights)


def attend_kernel(query_a, query_b, near, far, out, bias):
    rows = query_a.shape[0]
    blocks = 2 * near.shape[0]
    line, side = lax.axis_index("seq") // 2, lax.rem(lax.axis_index("seq"), 2)
    key_value = jnp.concatenate([(near, far)[b % 2][b // 2] for b in range(blocks)], axis=0)
    keys, values = key_value[:, :HD], key_value[:, HD:]
    down = lax.broadcasted_iota(jnp.int32, (rows, rows), 0)
    along = lax.broadcasted_iota(jnp.int32, (rows, rows), 1)
    for number, query in enumerate((query_a, query_b)):
        upper = lax.rem(side + number, 2)
        at = 2 * lax.axis_index("expert") + upper
        for b in range(blocks):
            k, m = b // 2, b % 2
            behind = 2 * lax.rem(line + blocks // 2 - k, blocks // 2) + lax.rem(side + m, 2)
            behind = (at - behind) * rows + down - along
            bias[:, b * rows : (b + 1) * rows] = jnp.where(
                (behind >= 0) & (behind < BAND), 0.0, -1e30
            )
        target = block_of(upper, rows)
        for h in range(query.shape[1] // HD):
            head = slice(h * HD, (h + 1) * HD)
            scores = lax.dot_general(
                query[:, head], keys, (((1,), (1,)), ((), ())), preferred_element_type=F32
            )
            scores = scores * HD ** (-0.5) + bias[...]
            probs = jnp.exp(scores - jnp.max(scores, axis=1, keepdims=True))
            total = jnp.sum(probs, axis=1, keepdims=True)
            mixed = jnp.dot(probs.astype(BF), values, preferred_element_type=F32)
            out[target, head] = (mixed / total).astype(BF)


def attended(query_a, query_b, near, far):
    rows, width = query_a.shape
    count = 2 * near.shape[0] * near.shape[1]
    return pl.pallas_call(
        attend_kernel,
        cost_estimate=LIGHT,
        out_shape=jax.ShapeDtypeStruct((2 * rows, width), BF),
        in_specs=[VMEM] * 4,
        out_specs=VMEM,
        scratch_shapes=[pltpu.VMEM((rows, count), F32)],
        compiler_params=pltpu.CompilerParams(vmem_limit_bytes=24 << 20),
    )(query_a, query_b, near, far)


def lane_body(
    tokens, expert_ids, route_weights, w_gate, w_up, w_down, query_rows, key_rows, value_rows
):
    seq_index = lax.axis_index("seq")
    expert_index = lax.axis_index("expert")
    lines = lax.axis_size("seq") // 2
    side = seq_index % 2
    lane, core = expert_index // 2, expert_index % 2
    rows, width = tokens.shape
    quarter = width // 4

    routes = {
        "core": pairs_of(lines, lambda l, s, n, c: (l, s, n, 1 - c)),
        "lane": pairs_of(lines, lambda l, s, n, c: (l, s, 1 - n, c)),
    }
    for k in range(lines):
        for m in range(2):
            routes[k, m] = pairs_of(
                lines, lambda l, s, n, c: ((l + k) % lines, (s + m) % 2, n, c)
            )
            routes["query", m] = pairs_of(
                lines, lambda l, s, n, c: (2 * c + n, (s + m) % 2, l // 2, l % 2)
            )
    flight = {}
    now = [jnp.zeros((), F32)]

    def at(value):
        value, now[0] = lax.optimization_barrier((value, now[0]))
        return value

    def start(name, value, route):
        with jax.named_scope("send_" + name):
            flight[name] = lax.ppermute(at(value), AXES, routes[route])

    def done(name):
        return at(flight.pop(name))

    own, opp, parts, moe = {}, {}, {}, {}
    half = rows // 2

    def expert_on(k):
        parts[k] = at(expert_terms([own[k], opp[k]], w_gate, w_up, wg, wu, w_down, wd))

    def to_side(k):
        summed = parts[k][2] + done(f"rx{k}").astype(F32)
        start(f"ry{k}", summed.astype(BF), (0, 1))

    def lane_start(k):
        start(f"rw{k}", parts[k][1], "lane")

    def lane_done(k):
        moe[k] = moe.get(k, parts[k][3]) + done(f"rw{k}").astype(F32)

    def side_done(k):
        moe[k] = moe.get(k, parts[k][3]) + done(f"ry{k}").astype(F32)

    own[0] = at(rows_of(tokens, expert_ids, route_weights))
    start("z1", own[0], (1, 0))
    start("y0", own[0], (0, 1))
    start("wg", w_gate, "core")
    start("wu", w_up, "core")
    *packets, query_a, query_b = at(
        packed(key_rows, value_rows, query_rows, (w_gate, w_up, w_down), lines)
    )
    start("kz1", packets[1], (1, 0))
    packets[1] = done("kz1")
    own[1] = done("z1")
    opp[0] = done("y0")
    wg = done("wg")
    wu = done("wu")
    start("z2", own[1], (1, 0))
    start("y1", own[1], (0, 1))
    start("wd", w_down, "core")
    start("q0", query_a, ("query", 0))
    wd = done("wd")
    expert_on(0)
    opp[1] = done("y1")
    own[2] = done("z2")
    query_a = done("q0")
    start("y2", own[2], (0, 1))
    start("z3", own[0], (3, 0))
    start("rx0", parts[0][0], "lane")
    for k in (2, 3):
        start(f"kz{k}", packets[k], (k, 0))
    expert_on(1)
    opp[2] = done("y2")
    own[3] = done("z3")
    for k in (2, 3):
        packets[k] = done(f"kz{k}")
    small = at(jnp.stack(packets))
    to_side(0)
    start("y3", own[3], (0, 1))
    start("rx1", parts[1][0], "lane")
    lane_start(1)
    start("q1", query_b, ("query", 1))
    expert_on(2)
    opp[3] = done("y3")
    start("rx2", parts[2][0], "lane")
    expert_on(3)
    side_done(0)
    lane_done(1)
    start("rx3", parts[3][0], "lane")
    to_side(1)
    to_side(2)
    lane_start(2)
    query_b = done("q1")
    start("ky", small, (0, 1))
    to_side(3)
    lane_start(3)
    side_done(1)
    start("rz1", moe[1].astype(BF), (3, 0))
    side_done(2)
    lane_done(2)
    start("rz2", moe[2].astype(BF), (1, 0))
    small_opp = done("ky")
    side_done(3)
    lane_done(3)
    lane_start(0)
    block = (moe[3] + done("rz2").astype(F32)).astype(BF)
    start("rz3", block, (1, 0))
    attn_out = at(attended(query_a, query_b, small, small_opp))
    lane_done(0)
    total = moe[0] + done("rz1").astype(F32)
    total = (total + done("rz3").astype(F32)).astype(BF)
    kept, passed = (cols(total, c * quarter, quarter) for c in (core, 1 - core))
    start("last", passed, "core")
    passed = done("last")
    moe_mixed = jnp.concatenate(
        [jnp.where(core == 0, kept, passed), jnp.where(core == 0, passed, kept)], axis=0
    )
    return (moe_mixed + now[0].astype(BF), attn_out)


def solution(mesh):
    placed = (
        P("seq", None),
        P("seq", None),
        P("seq", None),
        P(("seq", "expert"), None, None),
        P(("seq", "expert"), None, None),
        P(("seq", "expert"), None, None),
        P("seq", None),
        P("seq", None),
        P("seq", None),
    )
    fits = mesh.shape["expert"] == 4 and mesh.shape["seq"] == 8
    return jax.shard_map(
        lane_body if fits else general_body,
        mesh=mesh,
        in_specs=placed,
        out_specs=(P("seq", "expert"), P("expert", "seq")),
        check_vma=False,
    )
```
